32 devices in a mesh: row: 4 (over z), col: 8 (over y, x, core).
Axes of the slice: x: 2, y: 2, z: 4, core: 2. Of those that a mesh axis runs over, the one named last changes fastest.
Arguments:
- panel: bfloat16 [16, 1024, 256], P('row', 'col'), may hold values from -6 to 6
- inverse_factor: bfloat16 [1024, 1024], P('row', 'col'), as said below
- ranks: int32 [16], replicated, may hold values from 32 to 256
Outputs:
- solved: bfloat16 [16, 1024, 256], P('row', 'col')
- core_blocks: bfloat16 [16, 16, 256, 256], P('row', 'col')
The draws below stay inside these ranges and needn't reach their ends.
Inputs may be any that keep to these rules, and one draw needn't show every extreme that they name: inverse_factor is lower triangular with a diagonal between 0.5 and 3.
All inputs are finite; a program needn't handle non-finite values.
Results may differ from the reference program's by a relative error of at most 0.017.
Values may be sent and summed in bfloat16 or wider, within the bound.
A program may use at most 64 MiB of HBM per device.

```python
import math
import jax
import jax.numpy as jnp
from jax import lax

NB = 1024
RMAX = 256
TILES = 16
N_COL = 8


def draw_inverse_factor(key, part):
    key_lower = jax.random.fold_in(key, 11)
    key_diag = jax.random.fold_in(key, 12)
    lower_part = jax.random.normal(key_lower, (NB, NB), jnp.float32) * (1.0 / math.sqrt(NB))
    diagonal = jax.random.uniform(key_diag, (NB,), jnp.float32, minval=0.5, maxval=1.5)
    positions = jnp.arange(NB)
    matrix = jnp.where(positions[:, None] > positions[None, :], lower_part, 0.0) + jnp.diag(diagonal)
    return matrix.astype(jnp.bfloat16)


def place_ends(values, rng, smallest, high):
    longest = values.shape.index(max(values.shape))
    spots = []
    for shift in (0, 1):
        where = [jax.random.randint(jax.random.fold_in(rng, axis), (), 0, length) for axis, length in enumerate(values.shape)]
        where[longest] = (where[longest] + shift) % values.shape[longest]
        spots.append(tuple(where))
    return values.at[spots[0]].set(smallest).at[spots[1]].set(high)


def block_levels(key, dims, split, low, top_value):
    def one(dim, blocks):
        steps = jax.random.uniform(jax.random.fold_in(jax.random.fold_in(key, 6), dim), (blocks,), jnp.float32, low / len(split), top_value / len(split))
        return jnp.repeat(jnp.exp(steps), dims[dim] // blocks).reshape((-1,) + (1,) * (len(dims) - dim - 1))

    level = one(*split[0])
    for cut in split[1:]:
        level = level * one(*cut)
    return level


def gaussian(key, shape, width, limit, split=(), held_as=jnp.bfloat16):
    level = block_levels(key, shape, split, -0.22, 0.18) if split else 1.0
    entries = jax.random.normal(key, shape, jnp.float32) * width * level
    return jnp.minimum(jnp.maximum(entries, -limit), limit).astype(held_as)


def setup_inputs(seed: int = 0) -> dict:
    key_of = jax.random.split(jax.random.key(seed), 4)
    return {
        "panel": gaussian(key_of[0], (TILES, NB, RMAX), 1.0, 6.0, ((0, 4), (1, 8))),
        "inverse_factor": draw_inverse_factor(jax.random.fold_in(key_of[3], 71), 0),
        "ranks": place_ends(jax.random.randint(key_of[2], (TILES,), RMAX // 8, RMAX + 1), jax.random.fold_in(key_of[2], 1), RMAX // 8, RMAX).astype(jnp.int32),
    }


def reference(panel, inverse_factor, ranks):
    column_ids = jnp.arange(RMAX, dtype=jnp.int32)
    keep_cols = (column_ids[None, :] < ranks[:, None]).astype(jnp.bfloat16)
    masked = panel * keep_cols[:, None, :]
    slice_width = NB // N_COL

    def add_block(block_index, running):
        first = (block_index * slice_width).astype(jnp.int32)
        factor_part = lax.dynamic_slice_in_dim(inverse_factor, first, slice_width, 1).astype(jnp.float32)
        panel_part = lax.dynamic_slice_in_dim(masked, first, slice_width, 1).astype(jnp.float32)
        product = jnp.einsum('ab,tbr->tar', factor_part, panel_part, precision=lax.Precision.HIGHEST)
        rounded = lax.optimization_barrier(product.astype(jnp.bfloat16))
        return running + rounded.astype(jnp.float32)

    running = lax.fori_loop(0, N_COL, add_block, jnp.zeros((TILES, NB, RMAX), jnp.float32))
    solved = running.astype(jnp.bfloat16)
    solved_wide = solved.astype(jnp.float32)

    def pair_row(left):
        return jnp.einsum('ar,uas->urs', left, solved_wide, precision=lax.Precision.HIGHEST).astype(jnp.bfloat16)

    core_blocks = lax.map(pair_row, solved_wide)
    return solved, core_blocks
```

```python
import functools

import jax
import jax.numpy as jnp
from jax import lax
from jax.experimental import pallas as pl
from jax.experimental.pallas import tpu as pltpu
from jax.sharding import PartitionSpec as P

MESH = pl.DeviceIdType.MESH
FLIPS = (1, 2, 4)


def spread(value, axis, source):
    kept = jnp.where(lax.axis_index(axis) == source, value, 0).astype(value.dtype)
    return lax.psum(kept, axis)


def per_device(panel, inverse_factor, ranks):
    tile_count = panel.shape[0]
    row_part = panel.shape[1]
    rank_width = panel.shape[2]
    row_index = lax.axis_index("row")
    col_index = lax.axis_index("col")
    col_count = lax.axis_size("col")
    row_count = lax.axis_size("row")
    factor_cols = lax.all_gather(inverse_factor, "row", axis=0, tiled=True)
    own_ranks = lax.dynamic_slice_in_dim(ranks, row_index * tile_count, tile_count, 0)
    column_ids = jnp.arange(rank_width, dtype=jnp.int32)
    keep_cols = (column_ids[None, :] < own_ranks[:, None]).astype(jnp.bfloat16)
    masked = panel * keep_cols[:, None, :]
    partial_value = jnp.einsum(
        "ab,tbr->tar", factor_cols, masked, preferred_element_type=jnp.float32
    )
    summed = lax.psum(partial_value.astype(jnp.bfloat16), "col")
    solved_own = lax.dynamic_slice_in_dim(summed, col_index * row_part, row_part, 1)
    tiles_per_col = tile_count * row_count // col_count
    first_tile = col_index * tiles_per_col
    source = first_tile // tile_count
    offset = first_tile % tile_count
    picked = lax.dynamic_slice_in_dim(summed, offset, tiles_per_col, 0)
    col_tiles = spread(picked, "row", source)
    core_blocks = jnp.einsum(
        "tar,uas->turs", summed, col_tiles, preferred_element_type=jnp.float32
    ).astype(jnp.bfloat16)
    return (solved_own, core_blocks)


def kernel(
    rows, cols, ranks_ref, p_ref, f_ref, o_ref, core_ref,
    fb, pb, cb, sr, srt, sc,
    recv, send, zf_send, zc_recv, zc_send, loc,
):
    z = lax.axis_index("row")
    c = lax.axis_index("col")
    tiles, pr, width = p_ref.shape
    fr, fc = f_ref.shape
    per = tiles * rows // cols
    groups = tiles // per
    source = (c * per) // tiles
    group = ((c * per) % tiles) // per

    def at(m):
        out = c
        for bit in FLIPS:
            if (m // bit) % 2:
                out = out + bit * (1 - 2 * ((c // bit) % 2))
        return out

    up, down = z + 1 < rows, z >= 1

    barrier = pltpu.get_barrier_semaphore()
    for bit in FLIPS:
        pl.semaphore_signal(barrier, inc=1, device_id=(z, at(bit)), device_id_type=MESH)

    @pl.when(up)
    def _():
        pl.semaphore_signal(barrier, inc=1, device_id=(z + 1, c), device_id_type=MESH)

    @pl.when(down)
    def _():
        pl.semaphore_signal(barrier, inc=1, device_id=(z - 1, c), device_id_type=MESH)

    def f_view(s, j):
        return fb.at[pl.ds(pl.multiple_of(j * fr, fr), fr), pl.ds(pl.multiple_of(s * fc, fc), fc)]

    def p_view(s, g):
        return pb.at[pl.ds(g * per, per), pl.ds(pl.multiple_of(s * pr, pr), pr), :]

    def c_view(s):
        return cb.at[:, pl.ds(pl.multiple_of(s * pr, pr), pr), :]

    def exists(s, j):
        return (j + 1) * fr > s * fc

    def flip_copy(view, m, item, way):
        return pltpu.make_async_remote_copy(
            src_ref=view, dst_ref=view,
            send_sem=send.at[m // 2, item, way], recv_sem=recv.at[m ^ FLIPS[way], item],
            device_id=(z, at(FLIPS[way])), device_id_type=MESH,
        )

    def act(copy, start):
        if start:
            copy.start()
        else:
            copy.wait_send()

    def wait_recv(view, m, item):
        pltpu.make_async_remote_copy(
            src_ref=view, dst_ref=view,
            send_sem=send.at[0, item, 0], recv_sem=recv.at[m, item],
            device_id=(z, at(1)), device_id_type=MESH,
        ).wait_recv()

    def f_forward(m, j, start=True):
        view = f_view(at(m), j)
        if m == 0:
            act(flip_copy(view, m, j, 1), start)
            act(flip_copy(view, m, j, 2), start)
        elif m == 2:
            @pl.when(j % 2 == 0)
            def _():
                act(flip_copy(view, m, j, 2), start)
        elif m == 4:
            @pl.when(j % 2 == 1)
            def _():
                act(flip_copy(view, m, j, 1), start)
        act(flip_copy(view, m, j, 0), start)

    def p_forward(m, g, start=True):
        view = p_view(at(m), g)
        item = rows + g
        if m == 0:
            act(flip_copy(view, m, item, 1), start)
            act(flip_copy(view, m, item, 2), start)
        elif m == 2 and g % 2 == 0:
            act(flip_copy(view, m, item, 2), start)
        elif m == 4 and g % 2 == 1:
            act(flip_copy(view, m, item, 1), start)
        act(flip_copy(view, m, item, 0), start)

    def zf(j, start=True):
        view = f_view(c, j)
        for way, (go, to) in enumerate((((z >= j) & up, z + 1), ((z <= j) & down, z - 1))):
            @pl.when(go)
            def _():
                act(pltpu.make_async_remote_copy(
                    src_ref=view, dst_ref=view,
                    send_sem=zf_send.at[j, way], recv_sem=recv.at[0, j],
                    device_id=(to, c), device_id_type=MESH,
                ), start)

    def zc(m, view, start=True):
        for way, (go, to) in enumerate((((z >= source) & up, z + 1), ((z <= source) & down, z - 1))):
            @pl.when(go)
            def _():
                act(pltpu.make_async_remote_copy(
                    src_ref=view, dst_ref=c_view(at(m)),
                    send_sem=zc_send.at[m, way], recv_sem=zc_recv.at[m],
                    device_id=(to, c), device_id_type=MESH,
                ), start)

    def own_copy(m):
        return pltpu.make_async_copy(p_view(at(m), group), c_view(at(m)), loc.at[m])

    def from_source(m):
        @pl.when(z == source)
        def _():
            zc(m, p_view(at(m), group))
            own_copy(m).start()

    def relay(m):
        @pl.when(z != source)
        def _():
            view = c_view(at(m))
            pltpu.make_async_remote_copy(
                src_ref=view, dst_ref=view,
                send_sem=zc_send.at[m, 0], recv_sem=zc_recv.at[m],
                device_id=(z, at(1)), device_id_type=MESH,
            ).wait_recv()
            zc(m, view)

    f_view(c, z)[...] = f_ref[...]
    lanes = lax.broadcasted_iota(jnp.int32, (pr, width), 1)
    for t in range(tiles):
        keep = lanes < ranks_ref[z * tiles + t]
        pb[t, pl.ds(pl.multiple_of(c * pr, pr), pr), :] = jnp.where(
            keep, p_ref[t].astype(jnp.float32), 0.0
        ).astype(pb.dtype)

    pl.semaphore_wait(barrier, len(FLIPS) + jnp.where(up, 1, 0) + jnp.where(down, 1, 0))

    @pl.when(exists(c, z))
    def _():
        zf(z)
        f_forward(0, z)

    from_source(0)
    for g in range(groups):
        p_forward(0, g)

    def near_first(body):
        for d in range(1, rows):
            for j in (z + d, z - d):
                @pl.when((j >= 0) & (j < rows))
                def _():
                    @pl.when(exists(c, j))
                    def _():
                        body(j)

    def f_along(j):
        wait_recv(f_view(c, j), 0, j)
        zf(j)
        f_forward(0, j)

    near_first(f_along)

    def p_arrive(m):
        for g in range(groups):
            wait_recv(p_view(at(m), g), m, rows + g)
            if m % 2 == 0:
                p_forward(m, g)
        from_source(m)

    def f_arrive(m):
        def one(d, carry):
            j = (z + d) % rows

            @pl.when(exists(at(m), j))
            def _():
                wait_recv(f_view(at(m), j), m, j)
                if m % 2 == 0:
                    f_forward(m, j)

            return carry

        lax.fori_loop(0, rows, one, 0)

    p_arrive(1)
    relay(0)
    p_arrive(2)
    relay(1)
    p_arrive(4)
    p_arrive(3)
    f_arrive(2)
    f_arrive(4)
    relay(2)
    p_arrive(6)
    f_arrive(6)
    p_arrive(5)
    p_arrive(7)
    relay(3)
    for m in (1, 3, 5, 7):
        f_arrive(m)

    def solve(i, from_ref, t):
        high = (i + 1) * fr
        return jnp.dot(
            fb[i * fr : high, :high], from_ref[t, :high, :], preferred_element_type=jnp.float32
        )

    def solve_rows(i):
        def one(t, carry):
            part = solve(i, pb, t)
            sr[t, i * fr : (i + 1) * fr, :] = part.astype(sr.dtype)
            srt[t, :, i * fr : (i + 1) * fr] = part.T.astype(srt.dtype)
            return carry

        lax.fori_loop(0, tiles, one, 0)

    for i in range(rows):
        solve_rows(i)
        if 4 + i < cols:
            relay(4 + i)
    for t in range(tiles):
        o_ref[t] = sr[t, pl.ds(pl.multiple_of(c * pr, pr), pr), :]
    for m in range(4 + rows, cols):
        relay(m)

    for m in range(cols):
        @pl.when(z == source)
        def _():
            own_copy(m).wait()
    for i in range(rows):
        for u in range(per):
            sc[u, i * fr : (i + 1) * fr, :] = solve(i, cb, u).astype(sc.dtype)

    def cores(t, carry):
        for u in range(per):
            core_ref[t, u] = jnp.dot(
                srt[t], sc[u], preferred_element_type=jnp.float32
            ).astype(core_ref.dtype)
        return carry

    lax.fori_loop(0, tiles, cores, 0)

    @pl.when(exists(c, z))
    def _():
        zf(z, start=False)
        f_forward(0, z, start=False)

    def f_along_left(j):
        zf(j, start=False)
        f_forward(0, j, start=False)

    near_first(f_along_left)
    for m in range(0, cols, 2):
        for g in range(groups):
            p_forward(m, g, start=False)
        if m:
            def one(j, carry, m=m):
                @pl.when(exists(at(m), j))
                def _():
                    f_forward(m, j, start=False)

                return carry

            lax.fori_loop(0, rows, one, 0)
    for m in range(cols):
        @pl.when(z == source)
        def _(m=m):
            zc(m, p_view(at(m), group), start=False)

        @pl.when(z != source)
        def _(m=m):
            zc(m, c_view(at(m)), start=False)


def fits(rows, cols, panel, factor):
    tiles, pr, width = panel.shape
    fr, fc = factor.shape
    per = tiles * rows // cols
    return (
        cols == 2 ** len(FLIPS)
        and rows > 1
        and per > 0
        and tiles == 2 * per
        and pr == fc
        and pr % 16 == 0
        and fr % fc == 0
        and fc % 128 == 0
        and width % 128 == 0
        and rows * fr == cols * fc
    )


def on_device(rows, cols, panel, factor, ranks):
    if not fits(rows, cols, panel, factor):
        return per_device(panel, factor, ranks)
    tiles, pr, width = panel.shape
    fr, fc = factor.shape
    order = rows * fr
    per = tiles * rows // cols
    items = rows + tiles // per
    vmem = pl.BlockSpec(memory_space=pltpu.VMEM)
    dma = pltpu.SemaphoreType.DMA
    kept = panel.dtype
    return tuple(pl.pallas_call(
        functools.partial(kernel, rows, cols),
        out_shape=(
            jax.ShapeDtypeStruct(panel.shape, kept),
            jax.ShapeDtypeStruct((tiles, per, width, width), kept),
        ),
        in_specs=[pl.BlockSpec(memory_space=pltpu.SMEM), vmem, vmem],
        out_specs=(vmem, vmem),
        scratch_shapes=[
            pltpu.VMEM((order, order), kept),
            pltpu.VMEM((tiles, order, width), kept),
            pltpu.VMEM((per, order, width), kept),
            pltpu.VMEM((tiles, order, width), kept),
            pltpu.VMEM((tiles, width, order), kept),
            pltpu.VMEM((per, order, width), kept),
            dma((cols, items)),
            dma((cols // 2, items, len(FLIPS))),
            dma((rows, 2)),
            dma((cols,)),
            dma((cols, 2)),
            dma((cols,)),
        ],
        compiler_params=pltpu.CompilerParams(
            collective_id=0, has_side_effects=True, vmem_limit_bytes=40 * 2**20
        ),
    )(ranks, panel, factor))


def solution(mesh):
    return jax.shard_map(
        functools.partial(on_device, mesh.shape["row"], mesh.shape["col"]),
        mesh=mesh,
        in_specs=(P("row", "col", None), P("row", "col"), P()),
        out_specs=(P("row", "col", None), P("row", "col", None, None)),
        check_vma=False,
    )
```

```python
import functools

import jax
import jax.numpy as jnp
from jax import lax
from jax.experimental import pallas as pl
from jax.experimental.pallas import tpu as pltpu
from jax.sharding import PartitionSpec as P

MESH = pl.DeviceIdType.MESH
FLIPS = (1, 2, 4)


def spread(value, axis, source):
    kept = jnp.where(lax.axis_index(axis) == source, value, 0).astype(value.dtype)
    return lax.psum(kept, axis)


def per_device(panel, inverse_factor, ranks):
    tile_count = panel.shape[0]
    row_part = panel.shape[1]
    rank_width = panel.shape[2]
    row_index = lax.axis_index("row")
    col_index = lax.axis_index("col")
    col_count = lax.axis_size("col")
    row_count = lax.axis_size("row")
    factor_cols = lax.all_gather(inverse_factor, "row", axis=0, tiled=True)
    own_ranks = lax.dynamic_slice_in_dim(ranks, row_index * tile_count, tile_count, 0)
    column_ids = jnp.arange(rank_width, dtype=jnp.int32)
    keep_cols = (column_ids[None, :] < own_ranks[:, None]).astype(jnp.bfloat16)
    masked = panel * keep_cols[:, None, :]
    partial_value = jnp.einsum(
        "ab,tbr->tar", factor_cols, masked, preferred_element_type=jnp.float32
    )
    summed = lax.psum(partial_value.astype(jnp.bfloat16), "col")
    solved_own = lax.dynamic_slice_in_dim(summed, col_index * row_part, row_part, 1)
    tiles_per_col = tile_count * row_count // col_count
    first_tile = col_index * tiles_per_col
    source = first_tile // tile_count
    offset = first_tile % tile_count
    picked = lax.dynamic_slice_in_dim(summed, offset, tiles_per_col, 0)
    col_tiles = spread(picked, "row", source)
    core_blocks = jnp.einsum(
        "tar,uas->turs", summed, col_tiles, preferred_element_type=jnp.float32
    ).astype(jnp.bfloat16)
    return (solved_own, core_blocks)


def kernel(
    rows, cols, ranks_hbm, p_hbm, f_hbm, o_ref, core_ref,
    ranks_ref, p_ref, fb, pb, cb, sr, srt, wt, acc,
    recv, send, zf_send, zc_recv, zc_send, loc, fetch,
):
    z = lax.axis_index("row")
    c = lax.axis_index("col")
    tiles, pr, width = p_ref.shape
    fr, fc = f_hbm.shape
    per = tiles * rows // cols
    groups = tiles // per
    source = (c * per) // tiles
    group = ((c * per) % tiles) // per

    def at(m):
        out = c
        for bit in FLIPS:
            if (m // bit) % 2:
                out = out + bit * (1 - 2 * ((c // bit) % 2))
        return out

    up, down = z + 1 < rows, z >= 1

    fetches = (
        pltpu.make_async_copy(ranks_hbm, ranks_ref, fetch.at[0]),
        pltpu.make_async_copy(
            f_hbm,
            fb.at[pl.ds(pl.multiple_of(z * fr, fr), fr), pl.ds(pl.multiple_of(c * fc, fc), fc)],
            fetch.at[1],
        ),
        pltpu.make_async_copy(p_hbm, p_ref, fetch.at[2]),
    )
    for copy in fetches:
        copy.start()

    barrier = pltpu.get_barrier_semaphore()
    for bit in FLIPS:
        pl.semaphore_signal(barrier, inc=1, device_id=(z, at(bit)), device_id_type=MESH)

    @pl.when(up)
    def _():
        pl.semaphore_signal(barrier, inc=1, device_id=(z + 1, c), device_id_type=MESH)

    @pl.when(down)
    def _():
        pl.semaphore_signal(barrier, inc=1, device_id=(z - 1, c), device_id_type=MESH)

    def f_view(s, j):
        return fb.at[pl.ds(pl.multiple_of(j * fr, fr), fr), pl.ds(pl.multiple_of(s * fc, fc), fc)]

    def p_view(s, g):
        return pb.at[pl.ds(g * per, per), pl.ds(pl.multiple_of(s * pr, pr), pr), :]

    def p_tile(s, u):
        return pb.at[group * per + u, pl.ds(pl.multiple_of(s * pr, pr), pr), :]

    def c_tile(s, u):
        return cb.at[u, pl.ds(pl.multiple_of(s * pr, pr), pr), :]

    def exists(s, j):
        return (j + 1) * fr > s * fc

    def flip_copy(view, m, item, way):
        return pltpu.make_async_remote_copy(
            src_ref=view, dst_ref=view,
            send_sem=send.at[m // 2, item, way], recv_sem=recv.at[m ^ FLIPS[way], item],
            device_id=(z, at(FLIPS[way])), device_id_type=MESH,
        )

    def act(copy, start):
        if start:
            copy.start()
        else:
            copy.wait_send()

    def wait_recv(view, m, item):
        pltpu.make_async_remote_copy(
            src_ref=view, dst_ref=view,
            send_sem=send.at[0, item, 0], recv_sem=recv.at[m, item],
            device_id=(z, at(1)), device_id_type=MESH,
        ).wait_recv()

    def f_forward(m, j, start=True):
        view = f_view(at(m), j)
        if m == 0:
            act(flip_copy(view, m, j, 1), start)
            act(flip_copy(view, m, j, 2), start)
        elif m == 2:
            @pl.when(j % 2 == 0)
            def _():
                act(flip_copy(view, m, j, 2), start)
        elif m == 4:
            @pl.when(j % 2 == 1)
            def _():
                act(flip_copy(view, m, j, 1), start)
        act(flip_copy(view, m, j, 0), start)

    def p_forward(m, g, start=True):
        view = p_view(at(m), g)
        item = rows + g
        if m == 0:
            act(flip_copy(view, m, item, 1), start)
            act(flip_copy(view, m, item, 2), start)
        elif m == 2 and g % 2 == 0:
            act(flip_copy(view, m, item, 2), start)
        elif m == 4 and g % 2 == 1:
            act(flip_copy(view, m, item, 1), start)
        act(flip_copy(view, m, item, 0), start)

    def zf(j, start=True):
        view = f_view(c, j)
        for way, (go, to) in enumerate((((z >= j) & up, z + 1), ((z <= j) & down, z - 1))):
            @pl.when(go)
            def _():
                act(pltpu.make_async_remote_copy(
                    src_ref=view, dst_ref=view,
                    send_sem=zf_send.at[j, way], recv_sem=recv.at[0, j],
                    device_id=(to, c), device_id_type=MESH,
                ), start)

    def zc(m, u, view, start=True):
        for way, (go, to) in enumerate((((z >= source) & up, z + 1), ((z <= source) & down, z - 1))):
            @pl.when(go)
            def _():
                act(pltpu.make_async_remote_copy(
                    src_ref=view, dst_ref=c_tile(at(m), u),
                    send_sem=zc_send.at[m, u, way], recv_sem=zc_recv.at[m, u],
                    device_id=(to, c), device_id_type=MESH,
                ), start)

    def own_copy(m, u):
        return pltpu.make_async_copy(p_tile(at(m), u), c_tile(at(m), u), loc.at[m, u])

    def from_source(m):
        @pl.when(z == source)
        def _():
            for u in range(per):
                zc(m, u, p_tile(at(m), u))
            for u in range(per):
                own_copy(m, u).start()

    def relay(m):
        @pl.when(z != source)
        def _():
            for u in range(per):
                view = c_tile(at(m), u)
                pltpu.make_async_remote_copy(
                    src_ref=view, dst_ref=view,
                    send_sem=zc_send.at[m, u, 0], recv_sem=zc_recv.at[m, u],
                    device_id=(z, at(1)), device_id_type=MESH,
                ).wait_recv()
                zc(m, u, view)

    for copy in fetches:
        copy.wait()
    lanes = lax.broadcasted_iota(jnp.int32, (pr, width), 1)
    for t in range(tiles):
        keep = lanes < ranks_ref[z * tiles + t]
        pb[t, pl.ds(pl.multiple_of(c * pr, pr), pr), :] = jnp.where(
            keep, p_ref[t].astype(jnp.float32), 0.0
        ).astype(pb.dtype)

    pl.semaphore_wait(barrier, len(FLIPS) + jnp.where(up, 1, 0) + jnp.where(down, 1, 0))

    @pl.when(exists(c, z))
    def _():
        zf(z)
        f_forward(0, z)

    from_source(0)
    for g in range(groups):
        p_forward(0, g)

    def near_first(body):
        for d in range(1, rows):
            for j in (z + d, z - d):
                @pl.when((j >= 0) & (j < rows))
                def _():
                    @pl.when(exists(c, j))
                    def _():
                        body(j)

    def f_along(j):
        wait_recv(f_view(c, j), 0, j)
        zf(j)
        f_forward(0, j)

    near_first(f_along)

    def p_arrive(m):
        for g in range(groups):
            wait_recv(p_view(at(m), g), m, rows + g)
            if m % 2 == 0:
                p_forward(m, g)
        from_source(m)

    def f_arrive(m):
        def one(d, carry):
            j = (z + d) % rows

            @pl.when(exists(at(m), j))
            def _():
                wait_recv(f_view(at(m), j), m, j)
                if m % 2 == 0:
                    f_forward(m, j)

            return carry

        lax.fori_loop(0, rows, one, 0)

    def solve_rows(i):
        high = (i + 1) * fr

        def one(t, carry):
            part = jnp.dot(
                fb[i * fr : high, :high], pb[t, :high, :], preferred_element_type=jnp.float32
            )
            sr[t, i * fr : high, :] = part.astype(sr.dtype)
            srt[t, :, i * fr : high] = part.T.astype(srt.dtype)
            return carry

        lax.fori_loop(0, tiles, one, 0)

    def weigh(i):
        def one(t, carry):
            wt[i, t] = jnp.dot(
                srt[t, :, i * fr :],
                fb[i * fr :, i * fr : (i + 1) * fr],
                preferred_element_type=jnp.float32,
            ).astype(wt.dtype)
            return carry

        lax.fori_loop(0, tiles, one, 0)

    pieces = fr // pr
    last = cols - pieces

    def add_cores(m):
        q = at(m) // pieces

        @pl.when(z == source)
        def _():
            for k in range(pieces):
                for u in range(per):
                    own_copy(m + k, u).wait()

        def one(t, carry):
            for u in range(per):
                part = jnp.dot(
                    wt[q, t],
                    cb[u, pl.ds(pl.multiple_of(q * fr, fr), fr), :],
                    preferred_element_type=jnp.float32,
                )
                if m == 0:
                    acc[t, u] = part
                elif m < last:
                    acc[t, u] += part
                else:
                    core_ref[t, u] = (acc[t, u] + part).astype(core_ref.dtype)
            return carry

        lax.fori_loop(0, tiles, one, 0)

    p_arrive(1)
    relay(0)
    p_arrive(2)
    p_arrive(4)
    relay(1)
    p_arrive(3)
    f_arrive(2)
    f_arrive(4)
    relay(2)
    p_arrive(5)
    p_arrive(6)
    f_arrive(6)
    relay(4)
    p_arrive(7)
    for m in (1, 3, 5, 7):
        f_arrive(m)
    relay(3)
    for i in range(rows):
        solve_rows(i)
        if i == rows // 2 - 1:
            relay(5)
    for i in range(rows):
        weigh(i)
        if i == rows // 2 - 1:
            relay(6)
    for t in range(tiles):
        o_ref[t] = sr[t, pl.ds(pl.multiple_of(c * pr, pr), pr), :]
    for m in range(0, last, pieces):
        add_cores(m)
    relay(7)
    add_cores(last)

    @pl.when(exists(c, z))
    def _():
        zf(z, start=False)
        f_forward(0, z, start=False)

    def f_along_left(j):
        zf(j, start=False)
        f_forward(0, j, start=False)

    near_first(f_along_left)
    for m in range(0, cols, 2):
        for g in range(groups):
            p_forward(m, g, start=False)
        if m:
            def one(j, carry, m=m):
                @pl.when(exists(at(m), j))
                def _():
                    f_forward(m, j, start=False)

                return carry

            lax.fori_loop(0, rows, one, 0)
    for m in range(cols):
        for u in range(per):
            @pl.when(z == source)
            def _():
                zc(m, u, p_tile(at(m), u), start=False)

            @pl.when(z != source)
            def _():
                zc(m, u, c_tile(at(m), u), start=False)


def fits(rows, cols, panel, factor):
    tiles, pr, width = panel.shape
    fr, fc = factor.shape
    per = tiles * rows // cols
    return (
        cols == 2 ** len(FLIPS)
        and rows > 1
        and per > 0
        and tiles == 2 * per
        and pr == fc
        and pr % 16 == 0
        and fr == 2 * fc
        and fc % 128 == 0
        and width % 128 == 0
        and rows * fr == cols * fc
    )


def on_device(rows, cols, panel, factor, ranks):
    if not fits(rows, cols, panel, factor):
        return per_device(panel, factor, ranks)
    tiles, pr, width = panel.shape
    fr, fc = factor.shape
    order = rows * fr
    per = tiles * rows // cols
    items = rows + tiles // per
    vmem = pl.BlockSpec(memory_space=pltpu.VMEM)
    dma = pltpu.SemaphoreType.DMA
    kept = panel.dtype
    return tuple(pl.pallas_call(
        functools.partial(kernel, rows, cols),
        out_shape=(
            jax.ShapeDtypeStruct(panel.shape, kept),
            jax.ShapeDtypeStruct((tiles, per, width, width), kept),
        ),
        in_specs=[pl.BlockSpec(memory_space=pltpu.HBM)] * 3,
        out_specs=(vmem, vmem),
        scratch_shapes=[
            pltpu.SMEM(ranks.shape, ranks.dtype),
            pltpu.VMEM(panel.shape, kept),
            pltpu.VMEM((order, order), kept),
            pltpu.VMEM((tiles, order, width), kept),
            pltpu.VMEM((per, order, width), kept),
            pltpu.VMEM((tiles, order, width), kept),
            pltpu.VMEM((tiles, width, order), kept),
            pltpu.VMEM((rows, tiles, width, fr), kept),
            pltpu.VMEM((tiles, per, width, width), jnp.float32),
            dma((cols, items)),
            dma((cols // 2, items, len(FLIPS))),
            dma((rows, 2)),
            dma((cols, per)),
            dma((cols, per, 2)),
            dma((cols, per)),
            dma((3,)),
        ],
        compiler_params=pltpu.CompilerParams(
            collective_id=0, has_side_effects=True, vmem_limit_bytes=60 * 2**20
        ),
    )(ranks, panel, factor))


def solution(mesh):
    return jax.shard_map(
        functools.partial(on_device, mesh.shape["row"], mesh.shape["col"]),
        mesh=mesh,
        in_specs=(P("row", "col", None), P("row", "col"), P()),
        out_specs=(P("row", "col", None), P("row", "col", None, None)),
        check_vma=False,
    )
```

```python
import functools

import jax
import jax.numpy as jnp
from jax import lax
from jax.experimental import pallas as pl
from jax.experimental.pallas import tpu as pltpu
from jax.sharding import PartitionSpec as P

MESH = pl.DeviceIdType.MESH
FLIPS = (1, 2, 4)


def spread(value, axis, source):
    kept = jnp.where(lax.axis_index(axis) == source, value, 0).astype(value.dtype)
    return lax.psum(kept, axis)


def per_device(panel, inverse_factor, ranks):
    tile_count = panel.shape[0]
    row_part = panel.shape[1]
    rank_width = panel.shape[2]
    row_index = lax.axis_index("row")
    col_index = lax.axis_index("col")
    col_count = lax.axis_size("col")
    row_count = lax.axis_size("row")
    factor_cols = lax.all_gather(inverse_factor, "row", axis=0, tiled=True)
    own_ranks = lax.dynamic_slice_in_dim(ranks, row_index * tile_count, tile_count, 0)
    column_ids = jnp.arange(rank_width, dtype=jnp.int32)
    keep_cols = (column_ids[None, :] < own_ranks[:, None]).astype(jnp.bfloat16)
    masked = panel * keep_cols[:, None, :]
    partial_value = jnp.einsum(
        "ab,tbr->tar", factor_cols, masked, preferred_element_type=jnp.float32
    )
    summed = lax.psum(partial_value.astype(jnp.bfloat16), "col")
    solved_own = lax.dynamic_slice_in_dim(summed, col_index * row_part, row_part, 1)
    tiles_per_col = tile_count * row_count // col_count
    first_tile = col_index * tiles_per_col
    source = first_tile // tile_count
    offset = first_tile % tile_count
    picked = lax.dynamic_slice_in_dim(summed, offset, tiles_per_col, 0)
    col_tiles = spread(picked, "row", source)
    core_blocks = jnp.einsum(
        "tar,uas->turs", summed, col_tiles, preferred_element_type=jnp.float32
    ).astype(jnp.bfloat16)
    return (solved_own, core_blocks)


def kernel(
    rows, cols, ranks_hbm, p_hbm, f_hbm, o_ref, core_ref,
    ranks_ref, p_ref, fb, pb, cb, pt, srt, wt, acc,
    recv, send, zf_send, zc_recv, zc_send, loc, fetch,
):
    z = lax.axis_index("row")
    c = lax.axis_index("col")
    tiles, pr, width = p_ref.shape
    fr, fc = f_hbm.shape
    per = tiles * rows // cols
    groups = tiles // per
    source = (c * per) // tiles
    group = ((c * per) % tiles) // per

    def at(m):
        out = c
        for bit in FLIPS:
            if (m // bit) % 2:
                out = out + bit * (1 - 2 * ((c // bit) % 2))
        return out

    up, down = z + 1 < rows, z >= 1

    fetches = (
        pltpu.make_async_copy(ranks_hbm, ranks_ref, fetch.at[0]),
        pltpu.make_async_copy(
            f_hbm,
            fb.at[pl.ds(pl.multiple_of(z * fr, fr), fr), pl.ds(pl.multiple_of(c * fc, fc), fc)],
            fetch.at[1],
        ),
        pltpu.make_async_copy(p_hbm, p_ref, fetch.at[2]),
    )
    for copy in fetches:
        copy.start()

    barrier = pltpu.get_barrier_semaphore()
    for bit in FLIPS:
        pl.semaphore_signal(barrier, inc=1, device_id=(z, at(bit)), device_id_type=MESH)

    @pl.when(up)
    def _():
        pl.semaphore_signal(barrier, inc=1, device_id=(z + 1, c), device_id_type=MESH)

    @pl.when(down)
    def _():
        pl.semaphore_signal(barrier, inc=1, device_id=(z - 1, c), device_id_type=MESH)

    def f_view(s, j):
        return fb.at[pl.ds(pl.multiple_of(j * fr, fr), fr), pl.ds(pl.multiple_of(s * fc, fc), fc)]

    def p_view(s, g):
        return pb.at[pl.ds(g * per, per), pl.ds(pl.multiple_of(s * pr, pr), pr), :]

    def p_tile(s, u):
        return pb.at[group * per + u, pl.ds(pl.multiple_of(s * pr, pr), pr), :]

    def c_tile(s, u):
        return cb.at[u, pl.ds(pl.multiple_of(s * pr, pr), pr), :]

    def exists(s, j):
        return (j + 1) * fr > s * fc

    def flip_copy(view, m, item, way):
        return pltpu.make_async_remote_copy(
            src_ref=view, dst_ref=view,
            send_sem=send.at[m // 2, item, way], recv_sem=recv.at[m ^ FLIPS[way], item],
            device_id=(z, at(FLIPS[way])), device_id_type=MESH,
        )

    def act(copy, start):
        if start:
            copy.start()
        else:
            copy.wait_send()

    def wait_recv(view, m, item):
        pltpu.make_async_remote_copy(
            src_ref=view, dst_ref=view,
            send_sem=send.at[0, item, 0], recv_sem=recv.at[m, item],
            device_id=(z, at(1)), device_id_type=MESH,
        ).wait_recv()

    def f_forward(m, j, start=True):
        view = f_view(at(m), j)
        if m == 0:
            act(flip_copy(view, m, j, 1), start)
            act(flip_copy(view, m, j, 2), start)
        elif m == 2:
            @pl.when(j % 2 == 0)
            def _():
                act(flip_copy(view, m, j, 2), start)
        elif m == 4:
            @pl.when(j % 2 == 1)
            def _():
                act(flip_copy(view, m, j, 1), start)
        act(flip_copy(view, m, j, 0), start)

    def p_forward(m, g, start=True):
        view = p_view(at(m), g)
        item = rows + g
        if m == 0:
            act(flip_copy(view, m, item, 1), start)
            act(flip_copy(view, m, item, 2), start)
        elif m == 2 and g % 2 == 0:
            act(flip_copy(view, m, item, 2), start)
        elif m == 4 and g % 2 == 1:
            act(flip_copy(view, m, item, 1), start)
        act(flip_copy(view, m, item, 0), start)

    def zf(j, start=True):
        view = f_view(c, j)
        for way, (go, to) in enumerate((((z >= j) & up, z + 1), ((z <= j) & down, z - 1))):
            @pl.when(go)
            def _():
                act(pltpu.make_async_remote_copy(
                    src_ref=view, dst_ref=view,
                    send_sem=zf_send.at[j, way], recv_sem=recv.at[0, j],
                    device_id=(to, c), device_id_type=MESH,
                ), start)

    def zc(m, u, view, start=True):
        for way, (go, to) in enumerate((((z >= source) & up, z + 1), ((z <= source) & down, z - 1))):
            @pl.when(go)
            def _():
                act(pltpu.make_async_remote_copy(
                    src_ref=view, dst_ref=c_tile(at(m), u),
                    send_sem=zc_send.at[m, u, way], recv_sem=zc_recv.at[m, u],
                    device_id=(to, c), device_id_type=MESH,
                ), start)

    def own_copy(m, u):
        return pltpu.make_async_copy(p_tile(at(m), u), c_tile(at(m), u), loc.at[m, u])

    def from_source(m):
        @pl.when(z == source)
        def _():
            for u in range(per):
                zc(m, u, p_tile(at(m), u))
            for u in range(per):
                own_copy(m, u).start()

    def relay(m):
        @pl.when(z != source)
        def _():
            for u in range(per):
                view = c_tile(at(m), u)
                pltpu.make_async_remote_copy(
                    src_ref=view, dst_ref=view,
                    send_sem=zc_send.at[m, u, 0], recv_sem=zc_recv.at[m, u],
                    device_id=(z, at(1)), device_id_type=MESH,
                ).wait_recv()
                zc(m, u, view)

    for copy in fetches:
        copy.wait()
    lanes = lax.broadcasted_iota(jnp.int32, (pr, width), 1)
    for t in range(tiles):
        keep = lanes < ranks_ref[z * tiles + t]
        pb[t, pl.ds(pl.multiple_of(c * pr, pr), pr), :] = jnp.where(
            keep, p_ref[t].astype(jnp.float32), 0.0
        ).astype(pb.dtype)

    pl.semaphore_wait(barrier, len(FLIPS) + jnp.where(up, 1, 0) + jnp.where(down, 1, 0))

    @pl.when(exists(c, z))
    def _():
        zf(z)
        f_forward(0, z)

    from_source(0)
    for g in range(groups):
        p_forward(0, g)

    def near_first(body):
        for d in range(1, rows):
            for j in (z + d, z - d):
                @pl.when((j >= 0) & (j < rows))
                def _():
                    @pl.when(exists(c, j))
                    def _():
                        body(j)

    def f_along(j):
        wait_recv(f_view(c, j), 0, j)
        zf(j)
        f_forward(0, j)

    near_first(f_along)

    def p_arrive(m):
        for g in range(groups):
            wait_recv(p_view(at(m), g), m, rows + g)
            if m % 2 == 0:
                p_forward(m, g)
        from_source(m)

    def f_arrive(m):
        def one(d, carry):
            j = (z + d) % rows

            @pl.when(exists(at(m), j))
            def _():
                wait_recv(f_view(at(m), j), m, j)
                if m % 2 == 0:
                    f_forward(m, j)

            return carry

        lax.fori_loop(0, rows, one, 0)

    def flip(m):
        s = at(m)
        for t in range(tiles):
            piece = pb[t, pl.ds(pl.multiple_of(s * pr, pr), pr), :]
            pt[t * width : (t + 1) * width, pl.ds(pl.multiple_of(s * pr, pr), pr)] = piece.T

    def solve_rows(i):
        high = (i + 1) * fr
        srt[:, i * fr : high] = lax.dot_general(
            pt[:, :high], fb[i * fr : high, :high], (((1,), (1,)), ((), ())),
            preferred_element_type=jnp.float32,
        ).astype(srt.dtype)

    def weigh(i):
        wt[i] = jnp.dot(
            srt[:, i * fr :],
            fb[i * fr :, i * fr : (i + 1) * fr],
            preferred_element_type=jnp.float32,
        ).astype(wt.dtype)

    pieces = fr // pr
    last = cols - pieces

    def add_cores(m):
        q = at(m) // pieces

        @pl.when(z == source)
        def _():
            for k in range(pieces):
                for u in range(per):
                    own_copy(m + k, u).wait()

        for u in range(per):
            part = jnp.dot(
                wt[q], cb[u, pl.ds(pl.multiple_of(q * fr, fr), fr), :],
                preferred_element_type=jnp.float32,
            )
            if m == 0:
                acc[u] = part
            elif m < last:
                acc[u] += part
            else:
                total = (acc[u] + part).astype(core_ref.dtype)
                for t in range(tiles):
                    core_ref[t, u] = total[t * width : (t + 1) * width]

    flip(0)
    p_arrive(1)
    relay(0)
    flip(1)
    p_arrive(2)
    p_arrive(4)
    relay(1)
    p_arrive(3)
    f_arrive(2)
    f_arrive(4)
    relay(2)
    for m in (2, 3, 4):
        flip(m)
    p_arrive(5)
    p_arrive(6)
    f_arrive(6)
    relay(4)
    flip(5)
    flip(6)
    p_arrive(7)
    flip(7)
    for m in (1, 3, 5, 7):
        f_arrive(m)
    relay(3)
    for i in range(rows):
        solve_rows(i)
        if i == rows // 2 - 1:
            relay(5)
    for t in range(tiles):
        o_ref[t] = srt[t * width : (t + 1) * width, pl.ds(pl.multiple_of(c * pr, pr), pr)].T
    relay(6)
    for i in range(rows):
        weigh(i)
    relay(7)
    for m in range(0, cols, pieces):
        add_cores(m)

    @pl.when(exists(c, z))
    def _():
        zf(z, start=False)
        f_forward(0, z, start=False)

    def f_along_left(j):
        zf(j, start=False)
        f_forward(0, j, start=False)

    near_first(f_along_left)
    for m in range(0, cols, 2):
        for g in range(groups):
            p_forward(m, g, start=False)
        if m:
            def one(j, carry, m=m):
                @pl.when(exists(at(m), j))
                def _():
                    f_forward(m, j, start=False)

                return carry

            lax.fori_loop(0, rows, one, 0)
    for m in range(cols):
        for u in range(per):
            @pl.when(z == source)
            def _():
                zc(m, u, p_tile(at(m), u), start=False)

            @pl.when(z != source)
            def _():
                zc(m, u, c_tile(at(m), u), start=False)


def fits(rows, cols, panel, factor):
    tiles, pr, width = panel.shape
    fr, fc = factor.shape
    per = tiles * rows // cols
    return (
        cols == 2 ** len(FLIPS)
        and rows > 1
        and per > 0
        and tiles == 2 * per
        and pr == fc
        and pr % 16 == 0
        and fr == 2 * fc
        and fc % 128 == 0
        and width % 128 == 0
        and rows * fr == cols * fc
    )


def on_device(rows, cols, panel, factor, ranks):
    if not fits(rows, cols, panel, factor):
        return per_device(panel, factor, ranks)
    tiles, pr, width = panel.shape
    fr, fc = factor.shape
    order = rows * fr
    per = tiles * rows // cols
    items = rows + tiles // per
    vmem = pl.BlockSpec(memory_space=pltpu.VMEM)
    dma = pltpu.SemaphoreType.DMA
    kept = panel.dtype
    return tuple(pl.pallas_call(
        functools.partial(kernel, rows, cols),
        out_shape=(
            jax.ShapeDtypeStruct(panel.shape, kept),
            jax.ShapeDtypeStruct((tiles, per, width, width), kept),
        ),
        in_specs=[pl.BlockSpec(memory_space=pltpu.HBM)] * 3,
        out_specs=(vmem, vmem),
        scratch_shapes=[
            pltpu.SMEM(ranks.shape, ranks.dtype),
            pltpu.VMEM(panel.shape, kept),
            pltpu.VMEM((order, order), kept),
            pltpu.VMEM((tiles, order, width), kept),
            pltpu.VMEM((per, order, width), kept),
            pltpu.VMEM((tiles * width, order), kept),
            pltpu.VMEM((tiles * width, order), kept),
            pltpu.VMEM((rows, tiles * width, fr), kept),
            pltpu.VMEM((per, tiles * width, width), jnp.float32),
            dma((cols, items)),
            dma((cols // 2, items, len(FLIPS))),
            dma((rows, 2)),
            dma((cols, per)),
            dma((cols, per, 2)),
            dma((cols, per)),
            dma((3,)),
        ],
        compiler_params=pltpu.CompilerParams(
            collective_id=0, has_side_effects=True, vmem_limit_bytes=40 * 2**20
        ),
    )(ranks, panel, factor))


def solution(mesh):
    return jax.shard_map(
        functools.partial(on_device, mesh.shape["row"], mesh.shape["col"]),
        mesh=mesh,
        in_specs=(P("row", "col", None), P("row", "col"), P()),
        out_specs=(P("row", "col", None), P("row", "col", None, None)),
        check_vma=False,
    )
```

```python
import functools

import jax
import jax.numpy as jnp
from jax import lax
from jax.experimental import pallas as pl
from jax.experimental.pallas import tpu as pltpu
from jax.sharding import PartitionSpec as P

MESH = pl.DeviceIdType.MESH
FLIPS = (1, 2, 4)
SIDE = 1


def spread(value, axis, source):
    kept = jnp.where(lax.axis_index(axis) == source, value, 0).astype(value.dtype)
    return lax.psum(kept, axis)


def per_device(panel, inverse_factor, ranks):
    tile_count = panel.shape[0]
    row_part = panel.shape[1]
    rank_width = panel.shape[2]
    row_index = lax.axis_index("row")
    col_index = lax.axis_index("col")
    col_count = lax.axis_size("col")
    row_count = lax.axis_size("row")
    factor_cols = lax.all_gather(inverse_factor, "row", axis=0, tiled=True)
    own_ranks = lax.dynamic_slice_in_dim(ranks, row_index * tile_count, tile_count, 0)
    column_ids = jnp.arange(rank_width, dtype=jnp.int32)
    keep_cols = (column_ids[None, :] < own_ranks[:, None]).astype(jnp.bfloat16)
    masked = panel * keep_cols[:, None, :]
    partial_value = jnp.einsum(
        "ab,tbr->tar", factor_cols, masked, preferred_element_type=jnp.float32
    )
    summed = lax.psum(partial_value.astype(jnp.bfloat16), "col")
    solved_own = lax.dynamic_slice_in_dim(summed, col_index * row_part, row_part, 1)
    tiles_per_col = tile_count * row_count // col_count
    first_tile = col_index * tiles_per_col
    source = first_tile // tile_count
    offset = first_tile % tile_count
    picked = lax.dynamic_slice_in_dim(summed, offset, tiles_per_col, 0)
    col_tiles = spread(picked, "row", source)
    core_blocks = jnp.einsum(
        "tar,uas->turs", summed, col_tiles, preferred_element_type=jnp.float32
    ).astype(jnp.bfloat16)
    return (solved_own, core_blocks)


def kernel(
    rows, cols, ranks_hbm, p_hbm, f_hbm, o_ref, core_ref,
    ranks_ref, p_ref, fb, pb, cb, pt, srt, wt, acc,
    xb, recv, send, zf_send, zc_recv, zc_send, loc, fetch, xs_recv, xs_send, xd_send,
):
    z = lax.axis_index("row")
    c = lax.axis_index("col")
    tiles, pr, width = p_ref.shape
    fr, fc = f_hbm.shape
    per = tiles * rows // cols
    groups = tiles // per
    source = (c * per) // tiles
    group = ((c * per) % tiles) // per

    def at(m):
        out = c
        for bit in FLIPS:
            if (m // bit) % 2:
                out = out + bit * (1 - 2 * ((c // bit) % 2))
        return out

    up, down = z + 1 < rows, z >= 1

    fetches = (
        pltpu.make_async_copy(ranks_hbm, ranks_ref, fetch.at[0]),
        pltpu.make_async_copy(
            f_hbm,
            fb.at[pl.ds(pl.multiple_of(z * fr, fr), fr), pl.ds(pl.multiple_of(c * fc, fc), fc)],
            fetch.at[1],
        ),
        pltpu.make_async_copy(p_hbm, p_ref, fetch.at[2]),
    )
    for copy in fetches:
        copy.start()

    barrier = pltpu.get_barrier_semaphore()
    for m in range(1, cols):
        pl.semaphore_signal(barrier, inc=1, device_id=(z, at(m)), device_id_type=MESH)

    @pl.when(up)
    def _():
        pl.semaphore_signal(barrier, inc=1, device_id=(z + 1, c), device_id_type=MESH)

    @pl.when(down)
    def _():
        pl.semaphore_signal(barrier, inc=1, device_id=(z - 1, c), device_id_type=MESH)

    def f_view(s, j):
        return fb.at[pl.ds(pl.multiple_of(j * fr, fr), fr), pl.ds(pl.multiple_of(s * fc, fc), fc)]

    def p_view(s, g):
        return pb.at[pl.ds(g * per, per), pl.ds(pl.multiple_of(s * pr, pr), pr), :]

    def p_tile(s, u):
        return pb.at[group * per + u, pl.ds(pl.multiple_of(s * pr, pr), pr), :]

    def c_tile(s, u):
        return cb.at[u, pl.ds(pl.multiple_of(s * pr, pr), pr), :]

    def exists(s, j):
        return (j + 1) * fr > s * fc

    def flip_copy(view, m, item, way):
        return pltpu.make_async_remote_copy(
            src_ref=view, dst_ref=view,
            send_sem=send.at[m // 2, item, way], recv_sem=recv.at[m ^ FLIPS[way], item],
            device_id=(z, at(FLIPS[way])), device_id_type=MESH,
        )

    def act(copy, start):
        if start:
            copy.start()
        else:
            copy.wait_send()

    def wait_recv(view, m, item):
        pltpu.make_async_remote_copy(
            src_ref=view, dst_ref=view,
            send_sem=send.at[0, item, 0], recv_sem=recv.at[m, item],
            device_id=(z, at(1)), device_id_type=MESH,
        ).wait_recv()

    def f_forward(m, j, start=True):
        view = f_view(at(m), j)
        if m == 0:
            act(flip_copy(view, m, j, 1), start)
            act(flip_copy(view, m, j, 2), start)
        elif m == 2:
            @pl.when(j % 2 == 0)
            def _():
                act(flip_copy(view, m, j, 2), start)
        elif m == 4:
            @pl.when(j % 2 == 1)
            def _():
                act(flip_copy(view, m, j, 1), start)
        act(flip_copy(view, m, j, 0), start)

    def p_forward(m, g, start=True):
        view = p_view(at(m), g)
        item = rows + g
        if m == 0:
            act(flip_copy(view, m, item, 1), start)
            act(flip_copy(view, m, item, 2), start)
        elif m == 2 and g % 2 == 0:
            act(flip_copy(view, m, item, 2), start)
        elif m == 4 and g % 2 == 1:
            act(flip_copy(view, m, item, 1), start)
        act(flip_copy(view, m, item, 0), start)

    def zf(j, start=True):
        view = f_view(c, j)
        for way, (go, to) in enumerate((((z >= j) & up, z + 1), ((z <= j) & down, z - 1))):
            @pl.when(go)
            def _():
                act(pltpu.make_async_remote_copy(
                    src_ref=view, dst_ref=view,
                    send_sem=zf_send.at[j, way], recv_sem=recv.at[0, j],
                    device_id=(to, c), device_id_type=MESH,
                ), start)

    def zc(m, u, view, start=True):
        s = at(m)
        ways = (
            ((z >= source) & up & (s < cols - SIDE), z + 1),
            ((z <= source) & down & (s >= SIDE), z - 1),
        )
        for way, (go, to) in enumerate(ways):
            @pl.when(go)
            def _():
                act(pltpu.make_async_remote_copy(
                    src_ref=view, dst_ref=c_tile(at(m), u),
                    send_sem=zc_send.at[m, u, way], recv_sem=zc_recv.at[at(m), u],
                    device_id=(to, c), device_id_type=MESH,
                ), start)

    def own_copy(m, u):
        return pltpu.make_async_copy(p_tile(at(m), u), c_tile(at(m), u), loc.at[m, u])

    def from_source(m):
        @pl.when(z == source)
        def _():
            for u in range(per):
                zc(m, u, p_tile(at(m), u))
            for u in range(per):
                own_copy(m, u).start()

    def relay(m):
        @pl.when(z != source)
        def _():
            for u in range(per):
                view = c_tile(at(m), u)
                pltpu.make_async_remote_copy(
                    src_ref=view, dst_ref=view,
                    send_sem=zc_send.at[m, u, 0], recv_sem=zc_recv.at[at(m), u],
                    device_id=(z, at(1)), device_id_type=MESH,
                ).wait_recv()
                zc(m, u, view)

    carrier = (c < SIDE) | (c >= cols - SIDE)
    step = jnp.where(c < SIDE, -1, 1)
    onward = (z + step >= 0) & (z + step < rows)

    def x_view(j, g):
        return xb.at[j, pl.ds(g * per, per)]

    def x_pass(j, g, view, start=True):
        @pl.when(onward)
        def _():
            act(pltpu.make_async_remote_copy(
                src_ref=view, dst_ref=x_view(j, g),
                send_sem=xs_send.at[j, g], recv_sem=xs_recv.at[j, g],
                device_id=(z + step, c), device_id_type=MESH,
            ), start)

    def x_deliver(j, g, start=True):
        for u in range(per):
            act(pltpu.make_async_remote_copy(
                src_ref=xb.at[j, g * per + u], dst_ref=c_tile(c, u),
                send_sem=xd_send.at[j, g, u], recv_sem=zc_recv.at[c, u],
                device_id=(z, j * groups + g), device_id_type=MESH,
            ), start)

    def x_own(start=True):
        @pl.when(carrier)
        def _():
            for g in range(groups):
                x_pass(z, g, p_view(c, g), start)

    def x_along(d, start=True):
        j = z - step * d

        @pl.when(carrier & (j >= 0) & (j < rows))
        def _():
            for g in range(groups):
                view = x_view(j, g)
                if start:
                    pltpu.make_async_remote_copy(
                        src_ref=view, dst_ref=view,
                        send_sem=xs_send.at[j, g], recv_sem=xs_recv.at[j, g],
                        device_id=(z, at(1)), device_id_type=MESH,
                    ).wait_recv()
                x_pass(j, g, view, start)
                x_deliver(j, g, start)

    for copy in fetches:
        copy.wait()
    lanes = lax.broadcasted_iota(jnp.int32, (pr, width), 1)
    for t in range(tiles):
        keep = lanes < ranks_ref[z * tiles + t]
        pb[t, pl.ds(pl.multiple_of(c * pr, pr), pr), :] = jnp.where(
            keep, p_ref[t].astype(jnp.float32), 0.0
        ).astype(pb.dtype)

    pl.semaphore_wait(barrier, cols - 1 + jnp.where(up, 1, 0) + jnp.where(down, 1, 0))

    @pl.when(exists(c, z))
    def _():
        zf(z)
        f_forward(0, z)

    from_source(0)
    for g in range(groups):
        p_forward(0, g)
    x_own()

    def near_first(body):
        for d in range(1, rows):
            for j in (z + d, z - d):
                @pl.when((j >= 0) & (j < rows))
                def _():
                    @pl.when(exists(c, j))
                    def _():
                        body(j)

    def f_along(j):
        wait_recv(f_view(c, j), 0, j)
        zf(j)
        f_forward(0, j)

    near_first(f_along)

    def p_arrive(m):
        for g in range(groups):
            wait_recv(p_view(at(m), g), m, rows + g)
            if m % 2 == 0:
                p_forward(m, g)
        from_source(m)

    def f_arrive(m):
        def one(d, carry):
            j = (z + d) % rows

            @pl.when(exists(at(m), j))
            def _():
                wait_recv(f_view(at(m), j), m, j)
                if m % 2 == 0:
                    f_forward(m, j)

            return carry

        lax.fori_loop(0, rows, one, 0)

    def flip(m):
        s = at(m)
        for t in range(tiles):
            piece = pb[t, pl.ds(pl.multiple_of(s * pr, pr), pr), :]
            pt[t * width : (t + 1) * width, pl.ds(pl.multiple_of(s * pr, pr), pr)] = piece.T

    def solve_rows(i):
        high = (i + 1) * fr
        srt[:, i * fr : high] = lax.dot_general(
            pt[:, :high], fb[i * fr : high, :high], (((1,), (1,)), ((), ())),
            preferred_element_type=jnp.float32,
        ).astype(srt.dtype)

    def weigh(i):
        wt[i] = jnp.dot(
            srt[:, i * fr :],
            fb[i * fr :, i * fr : (i + 1) * fr],
            preferred_element_type=jnp.float32,
        ).astype(wt.dtype)

    pieces = fr // pr
    last = cols - pieces

    def add_cores(m):
        q = at(m) // pieces

        @pl.when(z == source)
        def _():
            for k in range(pieces):
                for u in range(per):
                    own_copy(m + k, u).wait()

        for u in range(per):
            part = jnp.dot(
                wt[q], cb[u, pl.ds(pl.multiple_of(q * fr, fr), fr), :],
                preferred_element_type=jnp.float32,
            )
            if m == 0:
                acc[u] = part
            elif m < last:
                acc[u] += part
            else:
                total = (acc[u] + part).astype(core_ref.dtype)
                for t in range(tiles):
                    core_ref[t, u] = total[t * width : (t + 1) * width]

    flip(0)
    p_arrive(1)
    relay(0)
    flip(1)
    p_arrive(2)
    p_arrive(4)
    relay(1)
    x_along(1)
    p_arrive(3)
    f_arrive(2)
    f_arrive(4)
    relay(2)
    for m in (2, 3, 4):
        flip(m)
    p_arrive(5)
    p_arrive(6)
    f_arrive(6)
    relay(4)
    x_along(2)
    flip(5)
    flip(6)
    p_arrive(7)
    flip(7)
    for m in (1, 3, 5, 7):
        f_arrive(m)
    relay(3)
    for d in range(3, rows):
        x_along(d)
    for i in range(rows):
        solve_rows(i)
    for t in range(tiles):
        o_ref[t] = srt[t * width : (t + 1) * width, pl.ds(pl.multiple_of(c * pr, pr), pr)].T
    relay(5)
    for i in range(rows):
        weigh(i)
    for m in range(0, last - pieces, pieces):
        add_cores(m)
    relay(6)
    add_cores(last - pieces)
    relay(7)
    add_cores(last)

    @pl.when(exists(c, z))
    def _():
        zf(z, start=False)
        f_forward(0, z, start=False)

    def f_along_left(j):
        zf(j, start=False)
        f_forward(0, j, start=False)

    near_first(f_along_left)
    x_own(start=False)
    for d in range(1, rows):
        x_along(d, start=False)
    for m in range(0, cols, 2):
        for g in range(groups):
            p_forward(m, g, start=False)
        if m:
            def one(j, carry, m=m):
                @pl.when(exists(at(m), j))
                def _():
                    f_forward(m, j, start=False)

                return carry

            lax.fori_loop(0, rows, one, 0)
    for m in range(cols):
        for u in range(per):
            @pl.when(z == source)
            def _():
                zc(m, u, p_tile(at(m), u), start=False)

            @pl.when(z != source)
            def _():
                zc(m, u, c_tile(at(m), u), start=False)


def fits(rows, cols, panel, factor):
    tiles, pr, width = panel.shape
    fr, fc = factor.shape
    per = tiles * rows // cols
    return (
        cols == 2 ** len(FLIPS)
        and rows > 1
        and per > 0
        and tiles == 2 * per
        and pr == fc
        and pr % 16 == 0
        and fr == 2 * fc
        and fc % 128 == 0
        and width % 128 == 0
        and rows * fr == cols * fc
    )


def on_device(rows, cols, panel, factor, ranks):
    if not fits(rows, cols, panel, factor):
        return per_device(panel, factor, ranks)
    tiles, pr, width = panel.shape
    fr, fc = factor.shape
    order = rows * fr
    per = tiles * rows // cols
    groups = tiles // per
    items = rows + groups
    vmem = pl.BlockSpec(memory_space=pltpu.VMEM)
    dma = pltpu.SemaphoreType.DMA
    kept = panel.dtype
    return tuple(pl.pallas_call(
        functools.partial(kernel, rows, cols),
        out_shape=(
            jax.ShapeDtypeStruct(panel.shape, kept),
            jax.ShapeDtypeStruct((tiles, per, width, width), kept),
        ),
        in_specs=[pl.BlockSpec(memory_space=pltpu.HBM)] * 3,
        out_specs=(vmem, vmem),
        scratch_shapes=[
            pltpu.SMEM(ranks.shape, ranks.dtype),
            pltpu.VMEM(panel.shape, kept),
            pltpu.VMEM((order, order), kept),
            pltpu.VMEM((tiles, order, width), kept),
            pltpu.VMEM((per, order, width), kept),
            pltpu.VMEM((tiles * width, order), kept),
            pltpu.VMEM((tiles * width, order), kept),
            pltpu.VMEM((rows, tiles * width, fr), kept),
            pltpu.VMEM((per, tiles * width, width), jnp.float32),
            pltpu.VMEM((rows,) + panel.shape, kept),
            dma((cols, items)),
            dma((cols // 2, items, len(FLIPS))),
            dma((rows, 2)),
            dma((cols, per)),
            dma((cols, per, 2)),
            dma((cols, per)),
            dma((3,)),
            dma((rows, groups)),
            dma((rows, groups)),
            dma((rows, groups, per)),
        ],
        compiler_params=pltpu.CompilerParams(
            collective_id=0, has_side_effects=True, vmem_limit_bytes=40 * 2**20
        ),
    )(ranks, panel, factor))


def solution(mesh):
    return jax.shard_map(
        functools.partial(on_device, mesh.shape["row"], mesh.shape["col"]),
        mesh=mesh,
        in_specs=(P("row", "col", None), P("row", "col"), P()),
        out_specs=(P("row", "col", None), P("row", "col", None, None)),
        check_vma=False,
    )
```

```python
import functools

import jax
import jax.numpy as jnp
from jax import lax
from jax.experimental import pallas as pl
from jax.experimental.pallas import tpu as pltpu
from jax.sharding import PartitionSpec as P

MESH = pl.DeviceIdType.MESH
FLIPS = (1, 2, 4)


def spread(value, axis, source):
    kept = jnp.where(lax.axis_index(axis) == source, value, 0).astype(value.dtype)
    return lax.psum(kept, axis)


def per_device(panel, inverse_factor, ranks):
    tile_count = panel.shape[0]
    row_part = panel.shape[1]
    rank_width = panel.shape[2]
    row_index = lax.axis_index("row")
    col_index = lax.axis_index("col")
    col_count = lax.axis_size("col")
    row_count = lax.axis_size("row")
    factor_cols = lax.all_gather(inverse_factor, "row", axis=0, tiled=True)
    own_ranks = lax.dynamic_slice_in_dim(ranks, row_index * tile_count, tile_count, 0)
    column_ids = jnp.arange(rank_width, dtype=jnp.int32)
    keep_cols = (column_ids[None, :] < own_ranks[:, None]).astype(jnp.bfloat16)
    masked = panel * keep_cols[:, None, :]
    partial_value = jnp.einsum(
        "ab,tbr->tar", factor_cols, masked, preferred_element_type=jnp.float32
    )
    summed = lax.psum(partial_value.astype(jnp.bfloat16), "col")
    solved_own = lax.dynamic_slice_in_dim(summed, col_index * row_part, row_part, 1)
    tiles_per_col = tile_count * row_count // col_count
    first_tile = col_index * tiles_per_col
    source = first_tile // tile_count
    offset = first_tile % tile_count
    picked = lax.dynamic_slice_in_dim(summed, offset, tiles_per_col, 0)
    col_tiles = spread(picked, "row", source)
    core_blocks = jnp.einsum(
        "tar,uas->turs", summed, col_tiles, preferred_element_type=jnp.float32
    ).astype(jnp.bfloat16)
    return (solved_own, core_blocks)


def kernel(
    rows, cols, ranks_hbm, p_hbm, f_hbm, o_ref, core_ref,
    ranks_ref, p_ref, fb, pb, cb, pt, srt, wt, acc,
    recv, send, zf_send, zc_recv, zc_send, loc, fetch, p_send, w_recv, w_send,
):
    z = lax.axis_index("row")
    c = lax.axis_index("col")
    tiles, pr, width = p_ref.shape
    fr, fc = f_hbm.shape
    per = tiles * rows // cols
    groups = tiles // per
    source = (c * per) // tiles
    group = ((c * per) % tiles) // per

    def at(m):
        out = c
        for bit in FLIPS:
            if (m // bit) % 2:
                out = out + bit * (1 - 2 * ((c // bit) % 2))
        return out

    up, down = z + 1 < rows, z >= 1

    fetches = (
        pltpu.make_async_copy(ranks_hbm, ranks_ref, fetch.at[0]),
        pltpu.make_async_copy(
            f_hbm,
            fb.at[pl.ds(pl.multiple_of(z * fr, fr), fr), pl.ds(pl.multiple_of(c * fc, fc), fc)],
            fetch.at[1],
        ),
        pltpu.make_async_copy(p_hbm, p_ref, fetch.at[2]),
    )
    for copy in fetches:
        copy.start()

    barrier = pltpu.get_barrier_semaphore()
    for bit in FLIPS:
        pl.semaphore_signal(barrier, inc=1, device_id=(z, at(bit)), device_id_type=MESH)

    @pl.when(up)
    def _():
        pl.semaphore_signal(barrier, inc=1, device_id=(z + 1, c), device_id_type=MESH)

    @pl.when(down)
    def _():
        pl.semaphore_signal(barrier, inc=1, device_id=(z - 1, c), device_id_type=MESH)

    def f_view(s, j):
        return fb.at[pl.ds(pl.multiple_of(j * fr, fr), fr), pl.ds(pl.multiple_of(s * fc, fc), fc)]

    def p_view(s, g):
        return pb.at[pl.ds(g * per, per), pl.ds(pl.multiple_of(s * pr, pr), pr), :]

    def p_tile(s, u):
        return pb.at[group * per + u, pl.ds(pl.multiple_of(s * pr, pr), pr), :]

    def c_tile(s, u):
        return cb.at[u, pl.ds(pl.multiple_of(s * pr, pr), pr), :]

    def exists(s, j):
        return (j + 1) * fr > s * fc

    def flip_copy(view, m, item, way):
        return pltpu.make_async_remote_copy(
            src_ref=view, dst_ref=view,
            send_sem=send.at[m // 2, item, way], recv_sem=recv.at[m ^ FLIPS[way], item],
            device_id=(z, at(FLIPS[way])), device_id_type=MESH,
        )

    def act(copy, start):
        if start:
            copy.start()
        else:
            copy.wait_send()

    def wait_recv(view, m, item):
        pltpu.make_async_remote_copy(
            src_ref=view, dst_ref=view,
            send_sem=send.at[0, item, 0], recv_sem=recv.at[m, item],
            device_id=(z, at(1)), device_id_type=MESH,
        ).wait_recv()

    def f_forward(m, j, start=True):
        view = f_view(at(m), j)
        if m == 0:
            act(flip_copy(view, m, j, 1), start)
            act(flip_copy(view, m, j, 2), start)
        elif m == 2:
            @pl.when(j % 2 == 0)
            def _():
                act(flip_copy(view, m, j, 2), start)
        elif m == 4:
            @pl.when(j % 2 == 1)
            def _():
                act(flip_copy(view, m, j, 1), start)
        act(flip_copy(view, m, j, 0), start)

    p_ways = {0: (1, 2), 1: (1, 2), 2: (2,), 5: (1,)}

    def p_forward(m, start=True):
        for way in p_ways.get(m, ()):
            view = p_view(at(m), group)
            act(pltpu.make_async_remote_copy(
                src_ref=view, dst_ref=view,
                send_sem=p_send.at[m, way], recv_sem=recv.at[m ^ FLIPS[way], rows],
                device_id=(z, at(FLIPS[way])), device_id_type=MESH,
            ), start)

    def p_swap(start=True):
        view = p_view(c, groups - 1 - group)
        act(pltpu.make_async_remote_copy(
            src_ref=view, dst_ref=view,
            send_sem=p_send.at[0, 0], recv_sem=recv.at[1, rows],
            device_id=(z, at(1)), device_id_type=MESH,
        ), start)

    def zf(j, start=True):
        view = f_view(c, j)
        for way, (go, to) in enumerate((((z >= j) & up, z + 1), ((z <= j) & down, z - 1))):
            @pl.when(go)
            def _():
                act(pltpu.make_async_remote_copy(
                    src_ref=view, dst_ref=view,
                    send_sem=zf_send.at[j, way], recv_sem=recv.at[0, j],
                    device_id=(to, c), device_id_type=MESH,
                ), start)

    def zc(m, u, view, start=True):
        for way, (go, to) in enumerate((((z >= source) & up, z + 1), ((z <= source) & down, z - 1))):
            @pl.when(go)
            def _():
                act(pltpu.make_async_remote_copy(
                    src_ref=view, dst_ref=c_tile(at(m), u),
                    send_sem=zc_send.at[m, u, way], recv_sem=zc_recv.at[m, u],
                    device_id=(to, c), device_id_type=MESH,
                ), start)

    def own_copy(m, u):
        return pltpu.make_async_copy(p_tile(at(m), u), c_tile(at(m), u), loc.at[m, u])

    def from_source(m):
        @pl.when(z == source)
        def _():
            for u in range(per):
                zc(m, u, p_tile(at(m), u))
            for u in range(per):
                own_copy(m, u).start()

    def relay(m):
        @pl.when(z != source)
        def _():
            for u in range(per):
                view = c_tile(at(m), u)
                pltpu.make_async_remote_copy(
                    src_ref=view, dst_ref=view,
                    send_sem=zc_send.at[m, u, 0], recv_sem=zc_recv.at[m, u],
                    device_id=(z, at(1)), device_id_type=MESH,
                ).wait_recv()
                zc(m, u, view)

    for copy in fetches:
        copy.wait()
    lanes = lax.broadcasted_iota(jnp.int32, (pr, width), 1)
    for t in range(tiles):
        keep = lanes < ranks_ref[z * tiles + t]
        pb[t, pl.ds(pl.multiple_of(c * pr, pr), pr), :] = jnp.where(
            keep, p_ref[t].astype(jnp.float32), 0.0
        ).astype(pb.dtype)

    pl.semaphore_wait(barrier, len(FLIPS) + jnp.where(up, 1, 0) + jnp.where(down, 1, 0))

    @pl.when(exists(c, z))
    def _():
        zf(z)
        f_forward(0, z)

    p_swap()
    from_source(0)
    p_forward(0)

    def near_first(body):
        for d in range(1, rows):
            for j in (z + d, z - d):
                @pl.when((j >= 0) & (j < rows))
                def _():
                    @pl.when(exists(c, j))
                    def _():
                        body(j)

    def f_along(j):
        wait_recv(f_view(c, j), 0, j)
        zf(j)
        f_forward(0, j)

    near_first(f_along)

    def p_arrive(m):
        wait_recv(p_view(at(m), group), m, rows)
        p_forward(m)
        from_source(m)

    def f_arrive(m):
        def one(d, carry):
            j = (z + d) % rows

            @pl.when(exists(at(m), j))
            def _():
                wait_recv(f_view(at(m), j), m, j)
                if m % 2 == 0:
                    f_forward(m, j)

            return carry

        lax.fori_loop(0, rows, one, 0)

    share = per * width
    half = pl.ds(pl.multiple_of(group * share, share), share)

    def flip(m):
        s = at(m)
        for u in range(per):
            piece = pb[group * per + u, pl.ds(pl.multiple_of(s * pr, pr), pr), :]
            pt[u * width : (u + 1) * width, pl.ds(pl.multiple_of(s * pr, pr), pr)] = piece.T

    def solve_rows(i):
        high = (i + 1) * fr
        srt[half, i * fr : high] = lax.dot_general(
            pt[:, :high], fb[i * fr : high, :high], (((1,), (1,)), ((), ())),
            preferred_element_type=jnp.float32,
        ).astype(srt.dtype)

    def weigh(i):
        wt[i, half, :] = jnp.dot(
            srt[half, i * fr :],
            fb[i * fr :, i * fr : (i + 1) * fr],
            preferred_element_type=jnp.float32,
        ).astype(wt.dtype)

    def swap(view, k):
        return pltpu.make_async_remote_copy(
            src_ref=view, dst_ref=view, send_sem=w_send.at[k], recv_sem=w_recv.at[k],
            device_id=(z, at(1)), device_id_type=MESH,
        )

    def w_swap(i):
        return swap(wt.at[i, half, :], i)

    def s_swap(s):
        return swap(srt.at[half, pl.ds(pl.multiple_of(s * pr, pr), pr)], rows)

    other = pl.ds(pl.multiple_of((groups - 1 - group) * share, share), share)

    pieces = fr // pr
    last = cols - pieces

    def add_cores(m):
        q = at(m) // pieces

        @pl.when(z == source)
        def _():
            for k in range(pieces):
                for u in range(per):
                    own_copy(m + k, u).wait()

        for u in range(per):
            part = jnp.dot(
                wt[q], cb[u, pl.ds(pl.multiple_of(q * fr, fr), fr), :],
                preferred_element_type=jnp.float32,
            )
            if m == 0:
                acc[u] = part
            elif m < last:
                acc[u] += part
            else:
                total = (acc[u] + part).astype(core_ref.dtype)
                for t in range(tiles):
                    core_ref[t, u] = total[t * width : (t + 1) * width]

    flip(0)
    p_arrive(1)
    relay(0)
    flip(1)
    p_arrive(2)
    p_arrive(4)
    relay(1)
    p_arrive(3)
    p_arrive(5)
    f_arrive(2)
    f_arrive(4)
    relay(2)
    p_arrive(6)
    p_arrive(7)
    f_arrive(6)
    for m in range(2, cols):
        flip(m)
    relay(4)
    for m in (1, 3, 5, 7):
        f_arrive(m)
    relay(3)
    for i in range(rows):
        solve_rows(i)
    s_swap(at(1)).start()
    relay(5)
    for i in range(rows):
        weigh(i)
        w_swap(i).start()
    swap(srt.at[other, pl.ds(pl.multiple_of(c * pr, pr), pr)], rows).wait_recv()
    for t in range(tiles):
        o_ref[t] = srt[t * width : (t + 1) * width, pl.ds(pl.multiple_of(c * pr, pr), pr)].T
    for i in range(rows):
        swap(wt.at[i, other, :], i).wait_recv()
    for m in range(0, last - pieces, pieces):
        add_cores(m)
    relay(6)
    add_cores(last - pieces)
    relay(7)
    add_cores(last)

    @pl.when(exists(c, z))
    def _():
        zf(z, start=False)
        f_forward(0, z, start=False)

    def f_along_left(j):
        zf(j, start=False)
        f_forward(0, j, start=False)

    near_first(f_along_left)
    p_swap(start=False)
    s_swap(at(1)).wait_send()
    for i in range(rows):
        w_swap(i).wait_send()
    for m in p_ways:
        p_forward(m, start=False)
    for m in range(0, cols, 2):
        if m:
            def one(j, carry, m=m):
                @pl.when(exists(at(m), j))
                def _():
                    f_forward(m, j, start=False)

                return carry

            lax.fori_loop(0, rows, one, 0)
    for m in range(cols):
        for u in range(per):
            @pl.when(z == source)
            def _():
                zc(m, u, p_tile(at(m), u), start=False)

            @pl.when(z != source)
            def _():
                zc(m, u, c_tile(at(m), u), start=False)


def fits(rows, cols, panel, factor):
    tiles, pr, width = panel.shape
    fr, fc = factor.shape
    per = tiles * rows // cols
    return (
        cols == 2 ** len(FLIPS)
        and rows > 1
        and per > 0
        and tiles == 2 * per
        and pr == fc
        and pr % 16 == 0
        and fr == 2 * fc
        and fc % 128 == 0
        and width % 128 == 0
        and rows * fr == cols * fc
    )


def on_device(rows, cols, panel, factor, ranks):
    if not fits(rows, cols, panel, factor):
        return per_device(panel, factor, ranks)
    tiles, pr, width = panel.shape
    fr, fc = factor.shape
    order = rows * fr
    per = tiles * rows // cols
    items = rows + 1
    vmem = pl.BlockSpec(memory_space=pltpu.VMEM)
    dma = pltpu.SemaphoreType.DMA
    kept = panel.dtype
    return tuple(pl.pallas_call(
        functools.partial(kernel, rows, cols),
        out_shape=(
            jax.ShapeDtypeStruct(panel.shape, kept),
            jax.ShapeDtypeStruct((tiles, per, width, width), kept),
        ),
        in_specs=[pl.BlockSpec(memory_space=pltpu.HBM)] * 3,
        out_specs=(vmem, vmem),
        scratch_shapes=[
            pltpu.SMEM(ranks.shape, ranks.dtype),
            pltpu.VMEM(panel.shape, kept),
            pltpu.VMEM((order, order), kept),
            pltpu.VMEM((tiles, order, width), kept),
            pltpu.VMEM((per, order, width), kept),
            pltpu.VMEM((per * width, order), kept),
            pltpu.VMEM((tiles * width, order), kept),
            pltpu.VMEM((rows, tiles * width, fr), kept),
            pltpu.VMEM((per, tiles * width, width), jnp.float32),
            dma((cols, items)),
            dma((cols // 2, items, len(FLIPS))),
            dma((rows, 2)),
            dma((cols, per)),
            dma((cols, per, 2)),
            dma((cols, per)),
            dma((3,)),
            dma((cols, len(FLIPS))),
            dma((rows + 1,)),
            dma((rows + 1,)),
        ],
        compiler_params=pltpu.CompilerParams(
            collective_id=0, has_side_effects=True, vmem_limit_bytes=40 * 2**20
        ),
    )(ranks, panel, factor))


def solution(mesh):
    return jax.shard_map(
        functools.partial(on_device, mesh.shape["row"], mesh.shape["col"]),
        mesh=mesh,
        in_specs=(P("row", "col", None), P("row", "col"), P()),
        out_specs=(P("row", "col", None), P("row", "col", None, None)),
        check_vma=False,
    )
```

```python
import functools

import jax
import jax.numpy as jnp
from jax import lax
from jax.experimental import pallas as pl
from jax.experimental.pallas import tpu as pltpu
from jax.sharding import PartitionSpec as P

MESH = pl.DeviceIdType.MESH
FLIPS = (1, 2, 4)


def spread(value, axis, source):
    kept = jnp.where(lax.axis_index(axis) == source, value, 0).astype(value.dtype)
    return lax.psum(kept, axis)


def per_device(panel, inverse_factor, ranks):
    tile_count = panel.shape[0]
    row_part = panel.shape[1]
    rank_width = panel.shape[2]
    row_index = lax.axis_index("row")
    col_index = lax.axis_index("col")
    col_count = lax.axis_size("col")
    row_count = lax.axis_size("row")
    factor_cols = lax.all_gather(inverse_factor, "row", axis=0, tiled=True)
    own_ranks = lax.dynamic_slice_in_dim(ranks, row_index * tile_count, tile_count, 0)
    column_ids = jnp.arange(rank_width, dtype=jnp.int32)
    keep_cols = (column_ids[None, :] < own_ranks[:, None]).astype(jnp.bfloat16)
    masked = panel * keep_cols[:, None, :]
    partial_value = jnp.einsum(
        "ab,tbr->tar", factor_cols, masked, preferred_element_type=jnp.float32
    )
    summed = lax.psum(partial_value.astype(jnp.bfloat16), "col")
    solved_own = lax.dynamic_slice_in_dim(summed, col_index * row_part, row_part, 1)
    tiles_per_col = tile_count * row_count // col_count
    first_tile = col_index * tiles_per_col
    source = first_tile // tile_count
    offset = first_tile % tile_count
    picked = lax.dynamic_slice_in_dim(summed, offset, tiles_per_col, 0)
    col_tiles = spread(picked, "row", source)
    core_blocks = jnp.einsum(
        "tar,uas->turs", summed, col_tiles, preferred_element_type=jnp.float32
    ).astype(jnp.bfloat16)
    return (solved_own, core_blocks)


def kernel(
    rows, cols, ranks_hbm, p_hbm, f_hbm, o_ref, core_ref,
    ranks_ref, p_ref, fb, pb, cb, pt, srt, wt, acc,
    recv, send, zf_send, zc_recv, zc_send, loc, fetch,
):
    z = lax.axis_index("row")
    c = lax.axis_index("col")
    tiles, pr, width = p_ref.shape
    fr, fc = f_hbm.shape
    per = tiles * rows // cols
    groups = tiles // per
    source = (c * per) // tiles
    group = ((c * per) % tiles) // per

    def at(m):
        out = c
        for bit in FLIPS:
            if (m // bit) % 2:
                out = out + bit * (1 - 2 * ((c // bit) % 2))
        return out

    up, down = z + 1 < rows, z >= 1

    fetches = (
        pltpu.make_async_copy(ranks_hbm, ranks_ref, fetch.at[0]),
        pltpu.make_async_copy(
            f_hbm,
            fb.at[c, pl.ds(pl.multiple_of(z * fr, fr), fr)],
            fetch.at[1],
        ),
        pltpu.make_async_copy(p_hbm, p_ref, fetch.at[2]),
    )
    for copy in fetches:
        copy.start()

    barrier = pltpu.get_barrier_semaphore()
    for bit in FLIPS:
        pl.semaphore_signal(barrier, inc=1, device_id=(z, at(bit)), device_id_type=MESH)

    @pl.when(up)
    def _():
        pl.semaphore_signal(barrier, inc=1, device_id=(z + 1, c), device_id_type=MESH)

    @pl.when(down)
    def _():
        pl.semaphore_signal(barrier, inc=1, device_id=(z - 1, c), device_id_type=MESH)

    def f_view(s, j):
        return fb.at[s, pl.ds(pl.multiple_of(j * fr, fr), fr)]

    def p_view(s, g):
        return pb.at[pl.ds(g * per, per), pl.ds(pl.multiple_of(s * pr, pr), pr), :]

    def p_tile(s, u):
        return pb.at[group * per + u, pl.ds(pl.multiple_of(s * pr, pr), pr), :]

    def c_tile(s, u):
        return cb.at[u, pl.ds(pl.multiple_of(s * pr, pr), pr), :]

    def exists(s, j):
        return (j + 1) * fr > s * fc

    def flip_copy(view, m, item, way):
        return pltpu.make_async_remote_copy(
            src_ref=view, dst_ref=view,
            send_sem=send.at[m // 2, item, way], recv_sem=recv.at[m ^ FLIPS[way], item],
            device_id=(z, at(FLIPS[way])), device_id_type=MESH,
        )

    def act(copy, start):
        if start:
            copy.start()
        else:
            copy.wait_send()

    def wait_recv(view, m, item):
        pltpu.make_async_remote_copy(
            src_ref=view, dst_ref=view,
            send_sem=send.at[0, item, 0], recv_sem=recv.at[m, item],
            device_id=(z, at(1)), device_id_type=MESH,
        ).wait_recv()

    def f_forward(m, j, start=True):
        view = f_view(at(m), j)
        if m == 0:
            act(flip_copy(view, m, j, 1), start)
            act(flip_copy(view, m, j, 2), start)
        elif m == 2:
            @pl.when(j % 2 == 0)
            def _():
                act(flip_copy(view, m, j, 2), start)
        elif m == 4:
            @pl.when(j % 2 == 1)
            def _():
                act(flip_copy(view, m, j, 1), start)
        act(flip_copy(view, m, j, 0), start)

    def p_forward(m, g, start=True):
        view = p_view(at(m), g)
        item = rows + g
        if m == 0:
            act(flip_copy(view, m, item, 1), start)
            act(flip_copy(view, m, item, 2), start)
        elif m == 2 and g % 2 == 0:
            act(flip_copy(view, m, item, 2), start)
        elif m == 4 and g % 2 == 1:
            act(flip_copy(view, m, item, 1), start)
        act(flip_copy(view, m, item, 0), start)

    def zf(j, start=True):
        view = f_view(c, j)
        for way, (go, to) in enumerate((((z >= j) & up, z + 1), ((z <= j) & down, z - 1))):
            @pl.when(go)
            def _():
                act(pltpu.make_async_remote_copy(
                    src_ref=view, dst_ref=view,
                    send_sem=zf_send.at[j, way], recv_sem=recv.at[0, j],
                    device_id=(to, c), device_id_type=MESH,
                ), start)

    def zc(m, u, view, start=True):
        for way, (go, to) in enumerate((((z >= source) & up, z + 1), ((z <= source) & down, z - 1))):
            @pl.when(go)
            def _():
                act(pltpu.make_async_remote_copy(
                    src_ref=view, dst_ref=c_tile(at(m), u),
                    send_sem=zc_send.at[m, u, way], recv_sem=zc_recv.at[m, u],
                    device_id=(to, c), device_id_type=MESH,
                ), start)

    def own_copy(m, u):
        return pltpu.make_async_copy(p_tile(at(m), u), c_tile(at(m), u), loc.at[m, u])

    def from_source(m):
        @pl.when(z == source)
        def _():
            for u in range(per):
                zc(m, u, p_tile(at(m), u))
            for u in range(per):
                own_copy(m, u).start()

    def relay(m):
        @pl.when(z != source)
        def _():
            for u in range(per):
                view = c_tile(at(m), u)
                pltpu.make_async_remote_copy(
                    src_ref=view, dst_ref=view,
                    send_sem=zc_send.at[m, u, 0], recv_sem=zc_recv.at[m, u],
                    device_id=(z, at(1)), device_id_type=MESH,
                ).wait_recv()
                zc(m, u, view)

    for copy in fetches:
        copy.wait()
    lanes = lax.broadcasted_iota(jnp.int32, (pr, width), 1)
    for t in range(tiles):
        keep = lanes < ranks_ref[z * tiles + t]
        pb[t, pl.ds(pl.multiple_of(c * pr, pr), pr), :] = jnp.where(
            keep, p_ref[t].astype(jnp.float32), 0.0
        ).astype(pb.dtype)

    pl.semaphore_wait(barrier, len(FLIPS) + jnp.where(up, 1, 0) + jnp.where(down, 1, 0))

    @pl.when(exists(c, z))
    def _():
        zf(z)
        f_forward(0, z)

    from_source(0)
    for g in range(groups):
        p_forward(0, g)

    def near_first(body):
        for d in range(1, rows):
            for j in (z + d, z - d):
                @pl.when((j >= 0) & (j < rows))
                def _():
                    @pl.when(exists(c, j))
                    def _():
                        body(j)

    def f_along(j):
        wait_recv(f_view(c, j), 0, j)
        zf(j)
        f_forward(0, j)

    near_first(f_along)

    def p_arrive(m):
        for g in range(groups):
            wait_recv(p_view(at(m), g), m, rows + g)
            if m % 2 == 0:
                p_forward(m, g)
        from_source(m)

    def f_arrive(m):
        def one(d, carry):
            j = (z + d) % rows

            @pl.when(exists(at(m), j))
            def _():
                wait_recv(f_view(at(m), j), m, j)
                if m % 2 == 0:
                    f_forward(m, j)

            return carry

        lax.fori_loop(0, rows, one, 0)

    def flip(m):
        s = at(m)
        for t in range(tiles):
            piece = pb[t, pl.ds(pl.multiple_of(s * pr, pr), pr), :]
            pt[t * width : (t + 1) * width, pl.ds(pl.multiple_of(s * pr, pr), pr)] = piece.T

    def solve_rows(i):
        high = (i + 1) * fr
        srt[:, i * fr : high] = lax.dot_general(
            pt[:, :high],
            jnp.concatenate([fb[k, i * fr : high] for k in range(high // fc)], axis=1),
            (((1,), (1,)), ((), ())),
            preferred_element_type=jnp.float32,
        ).astype(srt.dtype)

    def weigh(i):
        wt[i] = jnp.dot(
            srt[:, i * fr :],
            jnp.concatenate(
                [fb[k, i * fr :] for k in range(i * fr // fc, (i + 1) * fr // fc)], axis=1
            ),
            preferred_element_type=jnp.float32,
        ).astype(wt.dtype)

    pieces = fr // pr
    last = cols - pieces

    def add_cores(m):
        q = at(m) // pieces

        @pl.when(z == source)
        def _():
            for k in range(pieces):
                for u in range(per):
                    own_copy(m + k, u).wait()

        for u in range(per):
            part = jnp.dot(
                wt[q], cb[u, pl.ds(pl.multiple_of(q * fr, fr), fr), :],
                preferred_element_type=jnp.float32,
            )
            if m == 0:
                acc[u] = part
            elif m < last:
                acc[u] += part
            else:
                total = (acc[u] + part).astype(core_ref.dtype)
                for t in range(tiles):
                    core_ref[t, u] = total[t * width : (t + 1) * width]

    flip(0)
    p_arrive(1)
    relay(0)
    flip(1)
    p_arrive(2)
    p_arrive(4)
    relay(1)
    p_arrive(3)
    f_arrive(2)
    f_arrive(4)
    relay(2)
    for m in (2, 3, 4):
        flip(m)
    p_arrive(5)
    p_arrive(6)
    f_arrive(6)
    relay(4)
    flip(5)
    flip(6)
    p_arrive(7)
    flip(7)
    for m in (1, 3, 5, 7):
        f_arrive(m)
    relay(3)
    for i in range(rows):
        solve_rows(i)
        if i == rows // 2 - 1:
            relay(5)
    for t in range(tiles):
        o_ref[t] = srt[t * width : (t + 1) * width, pl.ds(pl.multiple_of(c * pr, pr), pr)].T
    relay(6)
    for i in range(rows):
        weigh(i)
    relay(7)
    for m in range(0, cols, pieces):
        add_cores(m)

    @pl.when(exists(c, z))
    def _():
        zf(z, start=False)
        f_forward(0, z, start=False)

    def f_along_left(j):
        zf(j, start=False)
        f_forward(0, j, start=False)

    near_first(f_along_left)
    for m in range(0, cols, 2):
        for g in range(groups):
            p_forward(m, g, start=False)
        if m:
            def one(j, carry, m=m):
                @pl.when(exists(at(m), j))
                def _():
                    f_forward(m, j, start=False)

                return carry

            lax.fori_loop(0, rows, one, 0)
    for m in range(cols):
        for u in range(per):
            @pl.when(z == source)
            def _():
                zc(m, u, p_tile(at(m), u), start=False)

            @pl.when(z != source)
            def _():
                zc(m, u, c_tile(at(m), u), start=False)


def fits(rows, cols, panel, factor):
    tiles, pr, width = panel.shape
    fr, fc = factor.shape
    per = tiles * rows // cols
    return (
        cols == 2 ** len(FLIPS)
        and rows > 1
        and per > 0
        and tiles == 2 * per
        and pr == fc
        and pr % 16 == 0
        and fr == 2 * fc
        and fc % 128 == 0
        and width % 128 == 0
        and rows * fr == cols * fc
    )


def on_device(rows, cols, panel, factor, ranks):
    if not fits(rows, cols, panel, factor):
        return per_device(panel, factor, ranks)
    tiles, pr, width = panel.shape
    fr, fc = factor.shape
    order = rows * fr
    per = tiles * rows // cols
    items = rows + tiles // per
    vmem = pl.BlockSpec(memory_space=pltpu.VMEM)
    dma = pltpu.SemaphoreType.DMA
    kept = panel.dtype
    return tuple(pl.pallas_call(
        functools.partial(kernel, rows, cols),
        out_shape=(
            jax.ShapeDtypeStruct(panel.shape, kept),
            jax.ShapeDtypeStruct((tiles, per, width, width), kept),
        ),
        in_specs=[pl.BlockSpec(memory_space=pltpu.HBM)] * 3,
        out_specs=(vmem, vmem),
        scratch_shapes=[
            pltpu.SMEM(ranks.shape, ranks.dtype),
            pltpu.VMEM(panel.shape, kept),
            pltpu.VMEM((cols, order, fc), kept),
            pltpu.VMEM((tiles, order, width), kept),
            pltpu.VMEM((per, order, width), kept),
            pltpu.VMEM((tiles * width, order), kept),
            pltpu.VMEM((tiles * width, order), kept),
            pltpu.VMEM((rows, tiles * width, fr), kept),
            pltpu.VMEM((per, tiles * width, width), jnp.float32),
            dma((cols, items)),
            dma((cols // 2, items, len(FLIPS))),
            dma((rows, 2)),
            dma((cols, per)),
            dma((cols, per, 2)),
            dma((cols, per)),
            dma((3,)),
        ],
        compiler_params=pltpu.CompilerParams(
            collective_id=0, has_side_effects=True, vmem_limit_bytes=40 * 2**20
        ),
    )(ranks, panel, factor))


def solution(mesh):
    return jax.shard_map(
        functools.partial(on_device, mesh.shape["row"], mesh.shape["col"]),
        mesh=mesh,
        in_specs=(P("row", "col", None), P("row", "col"), P()),
        out_specs=(P("row", "col", None), P("row", "col", None, None)),
        check_vma=False,
    )
```

```python
import functools

import jax
import jax.numpy as jnp
from jax import lax
from jax.experimental import pallas as pl
from jax.experimental.pallas import tpu as pltpu
from jax.sharding import PartitionSpec as P

MESH = pl.DeviceIdType.MESH
FLIPS = (1, 2, 4)


def spread(value, axis, source):
    kept = jnp.where(lax.axis_index(axis) == source, value, 0).astype(value.dtype)
    return lax.psum(kept, axis)


def per_device(panel, inverse_factor, ranks):
    tile_count = panel.shape[0]
    row_part = panel.shape[1]
    rank_width = panel.shape[2]
    row_index = lax.axis_index("row")
    col_index = lax.axis_index("col")
    col_count = lax.axis_size("col")
    row_count = lax.axis_size("row")
    factor_cols = lax.all_gather(inverse_factor, "row", axis=0, tiled=True)
    own_ranks = lax.dynamic_slice_in_dim(ranks, row_index * tile_count, tile_count, 0)
    column_ids = jnp.arange(rank_width, dtype=jnp.int32)
    keep_cols = (column_ids[None, :] < own_ranks[:, None]).astype(jnp.bfloat16)
    masked = panel * keep_cols[:, None, :]
    partial_value = jnp.einsum(
        "ab,tbr->tar", factor_cols, masked, preferred_element_type=jnp.float32
    )
    summed = lax.psum(partial_value.astype(jnp.bfloat16), "col")
    solved_own = lax.dynamic_slice_in_dim(summed, col_index * row_part, row_part, 1)
    tiles_per_col = tile_count * row_count // col_count
    first_tile = col_index * tiles_per_col
    source = first_tile // tile_count
    offset = first_tile % tile_count
    picked = lax.dynamic_slice_in_dim(summed, offset, tiles_per_col, 0)
    col_tiles = spread(picked, "row", source)
    core_blocks = jnp.einsum(
        "tar,uas->turs", summed, col_tiles, preferred_element_type=jnp.float32
    ).astype(jnp.bfloat16)
    return (solved_own, core_blocks)


def kernel(
    rows, cols, ranks_hbm, p_hbm, f_hbm, o_ref, core_ref,
    ranks_ref, p_ref, fb, pb, cb, pt, srt, wt, acc,
    recv, send, zf_send, zc_recv, zc_send, loc, fetch,
):
    z = lax.axis_index("row")
    c = lax.axis_index("col")
    tiles, pr, width = p_ref.shape
    fr, fc = f_hbm.shape
    per = tiles * rows // cols
    groups = tiles // per
    source = (c * per) // tiles
    group = ((c * per) % tiles) // per

    def at(m):
        out = c
        for bit in FLIPS:
            if (m // bit) % 2:
                out = out + bit * (1 - 2 * ((c // bit) % 2))
        return out

    up, down = z + 1 < rows, z >= 1

    fetches = (
        pltpu.make_async_copy(ranks_hbm, ranks_ref, fetch.at[0]),
        pltpu.make_async_copy(
            f_hbm,
            fb.at[c, pl.ds(pl.multiple_of(z * fr, fr), fr)],
            fetch.at[1],
        ),
        pltpu.make_async_copy(p_hbm, p_ref, fetch.at[2]),
    )
    for copy in fetches:
        copy.start()

    barrier = pltpu.get_barrier_semaphore()
    for bit in FLIPS:
        pl.semaphore_signal(barrier, inc=1, device_id=(z, at(bit)), device_id_type=MESH)

    @pl.when(up)
    def _():
        pl.semaphore_signal(barrier, inc=1, device_id=(z + 1, c), device_id_type=MESH)

    @pl.when(down)
    def _():
        pl.semaphore_signal(barrier, inc=1, device_id=(z - 1, c), device_id_type=MESH)

    def f_view(s, j):
        return fb.at[s, pl.ds(pl.multiple_of(j * fr, fr), fr)]

    def p_view(s, g):
        return pb.at[pl.ds(g * per, per), pl.ds(pl.multiple_of(s * pr, pr), pr), :]

    def p_tile(s, u):
        return pb.at[group * per + u, pl.ds(pl.multiple_of(s * pr, pr), pr), :]

    def c_tile(s, u):
        return cb.at[u, pl.ds(pl.multiple_of(s * pr, pr), pr), :]

    def exists(s, j):
        return (j + 1) * fr > s * fc

    def flip_copy(view, m, item, way):
        return pltpu.make_async_remote_copy(
            src_ref=view, dst_ref=view,
            send_sem=send.at[m // 2, item, way], recv_sem=recv.at[m ^ FLIPS[way], item],
            device_id=(z, at(FLIPS[way])), device_id_type=MESH,
        )

    def act(copy, start):
        if start:
            copy.start()
        else:
            copy.wait_send()

    def wait_recv(view, m, item):
        pltpu.make_async_remote_copy(
            src_ref=view, dst_ref=view,
            send_sem=send.at[0, item, 0], recv_sem=recv.at[m, item],
            device_id=(z, at(1)), device_id_type=MESH,
        ).wait_recv()

    def f_forward(m, j, start=True):
        view = f_view(at(m), j)
        if m == 0:
            act(flip_copy(view, m, j, 1), start)
            act(flip_copy(view, m, j, 2), start)
        elif m == 2:
            @pl.when(j % 2 == 0)
            def _():
                act(flip_copy(view, m, j, 2), start)
        elif m == 4:
            @pl.when(j % 2 == 1)
            def _():
                act(flip_copy(view, m, j, 1), start)
        act(flip_copy(view, m, j, 0), start)

    def p_forward(m, g, start=True):
        view = p_view(at(m), g)
        item = rows + g
        if m == 0:
            act(flip_copy(view, m, item, 1), start)
            act(flip_copy(view, m, item, 2), start)
        elif m == 2 and g % 2 == 0:
            act(flip_copy(view, m, item, 2), start)
        elif m == 4 and g % 2 == 1:
            act(flip_copy(view, m, item, 1), start)
        act(flip_copy(view, m, item, 0), start)

    def zf(j, start=True):
        view = f_view(c, j)
        for way, (go, to) in enumerate((((z >= j) & up, z + 1), ((z <= j) & down, z - 1))):
            @pl.when(go)
            def _():
                act(pltpu.make_async_remote_copy(
                    src_ref=view, dst_ref=view,
                    send_sem=zf_send.at[j, way], recv_sem=recv.at[0, j],
                    device_id=(to, c), device_id_type=MESH,
                ), start)

    def zc(m, u, view, start=True):
        for way, (go, to) in enumerate((((z >= source) & up, z + 1), ((z <= source) & down, z - 1))):
            @pl.when(go)
            def _():
                act(pltpu.make_async_remote_copy(
                    src_ref=view, dst_ref=c_tile(at(m), u),
                    send_sem=zc_send.at[m, u, way], recv_sem=zc_recv.at[m, u],
                    device_id=(to, c), device_id_type=MESH,
                ), start)

    def own_copy(m, u):
        return pltpu.make_async_copy(p_tile(at(m), u), c_tile(at(m), u), loc.at[m, u])

    def from_source(m):
        @pl.when(z == source)
        def _():
            for u in range(per):
                zc(m, u, p_tile(at(m), u))
            for u in range(per):
                own_copy(m, u).start()

    def relay(m):
        @pl.when(z != source)
        def _():
            for u in range(per):
                view = c_tile(at(m), u)
                pltpu.make_async_remote_copy(
                    src_ref=view, dst_ref=view,
                    send_sem=zc_send.at[m, u, 0], recv_sem=zc_recv.at[m, u],
                    device_id=(z, at(1)), device_id_type=MESH,
                ).wait_recv()
                zc(m, u, view)

    for copy in fetches:
        copy.wait()
    lanes = lax.broadcasted_iota(jnp.int32, (pr, width), 1)
    for t in range(tiles):
        keep = lanes < ranks_ref[z * tiles + t]
        pb[t, pl.ds(pl.multiple_of(c * pr, pr), pr), :] = jnp.where(
            keep, p_ref[t].astype(jnp.float32), 0.0
        ).astype(pb.dtype)

    pl.semaphore_wait(barrier, len(FLIPS) + jnp.where(up, 1, 0) + jnp.where(down, 1, 0))

    @pl.when(exists(c, z))
    def _():
        zf(z)
        f_forward(0, z)

    from_source(0)
    for g in range(groups):
        p_forward(0, g)

    def near_first(body):
        for d in range(1, rows):
            for j in (z + d, z - d):
                @pl.when((j >= 0) & (j < rows))
                def _():
                    @pl.when(exists(c, j))
                    def _():
                        body(j)

    def f_along(j):
        wait_recv(f_view(c, j), 0, j)
        zf(j)
        f_forward(0, j)

    near_first(f_along)

    def p_arrive(m):
        for g in range(groups):
            wait_recv(p_view(at(m), g), m, rows + g)
            if m % 2 == 0:
                p_forward(m, g)
        from_source(m)

    def f_arrive(m):
        def one(d, carry):
            j = (z + d) % rows

            @pl.when(exists(at(m), j))
            def _():
                wait_recv(f_view(at(m), j), m, j)
                if m % 2 == 0:
                    f_forward(m, j)

            return carry

        lax.fori_loop(0, rows, one, 0)

    def flip(m):
        s = at(m)
        for t in range(tiles):
            piece = pb[t, pl.ds(pl.multiple_of(s * pr, pr), pr), :]
            pt[t * width : (t + 1) * width, pl.ds(pl.multiple_of(s * pr, pr), pr)] = piece.T

    def solve_rows(i):
        high = (i + 1) * fr
        srt[:, i * fr : high] = lax.dot_general(
            pt[:, :high],
            jnp.concatenate([fb[k, i * fr : high] for k in range(high // fc)], axis=1),
            (((1,), (1,)), ((), ())),
            preferred_element_type=jnp.float32,
        ).astype(srt.dtype)

    def weigh(i):
        wt[i] = jnp.dot(
            srt[:, i * fr :],
            jnp.concatenate(
                [fb[k, i * fr :] for k in range(i * fr // fc, (i + 1) * fr // fc)], axis=1
            ),
            preferred_element_type=jnp.float32,
        ).astype(wt.dtype)

    pieces = fr // pr
    last = cols - pieces

    def add_cores(m):
        q = at(m) // pieces

        @pl.when(z == source)
        def _():
            for k in range(pieces):
                for u in range(per):
                    own_copy(m + k, u).wait()

        for u in range(per):
            part = jnp.dot(
                wt[q], cb[u, pl.ds(pl.multiple_of(q * fr, fr), fr), :],
                preferred_element_type=jnp.float32,
            )
            if m == 0:
                acc[u] = part
            elif m < last:
                acc[u] += part
            else:
                total = (acc[u] + part).astype(core_ref.dtype)
                for t in range(tiles):
                    core_ref[t, u] = total[t * width : (t + 1) * width]

    flip(0)
    p_arrive(1)
    relay(0)
    flip(1)
    p_arrive(2)
    p_arrive(4)
    relay(1)
    p_arrive(3)
    f_arrive(2)
    f_arrive(4)
    relay(2)
    for m in (2, 3, 4):
        flip(m)
    p_arrive(5)
    relay(4)
    p_arrive(6)
    f_arrive(6)
    p_arrive(7)
    relay(3)
    for m in (5, 6, 7):
        flip(m)
    for m in (1, 3, 5, 7):
        f_arrive(m)
    relay(5)
    for i in range(rows):
        solve_rows(i)
    relay(6)
    for t in range(tiles):
        o_ref[t] = srt[t * width : (t + 1) * width, pl.ds(pl.multiple_of(c * pr, pr), pr)].T
    for i in range(rows):
        weigh(i)
    relay(7)
    for m in range(0, cols, pieces):
        add_cores(m)

    @pl.when(exists(c, z))
    def _():
        zf(z, start=False)
        f_forward(0, z, start=False)

    def f_along_left(j):
        zf(j, start=False)
        f_forward(0, j, start=False)

    near_first(f_along_left)
    for m in range(0, cols, 2):
        for g in range(groups):
            p_forward(m, g, start=False)
        if m:
            def one(j, carry, m=m):
                @pl.when(exists(at(m), j))
                def _():
                    f_forward(m, j, start=False)

                return carry

            lax.fori_loop(0, rows, one, 0)
    for m in range(cols):
        for u in range(per):
            @pl.when(z == source)
            def _():
                zc(m, u, p_tile(at(m), u), start=False)

            @pl.when(z != source)
            def _():
                zc(m, u, c_tile(at(m), u), start=False)


def fits(rows, cols, panel, factor):
    tiles, pr, width = panel.shape
    fr, fc = factor.shape
    per = tiles * rows // cols
    return (
        cols == 2 ** len(FLIPS)
        and rows > 1
        and per > 0
        and tiles == 2 * per
        and pr == fc
        and pr % 16 == 0
        and fr == 2 * fc
        and fc % 128 == 0
        and width % 128 == 0
        and rows * fr == cols * fc
    )


def on_device(rows, cols, panel, factor, ranks):
    if not fits(rows, cols, panel, factor):
        return per_device(panel, factor, ranks)
    tiles, pr, width = panel.shape
    fr, fc = factor.shape
    order = rows * fr
    per = tiles * rows // cols
    items = rows + tiles // per
    vmem = pl.BlockSpec(memory_space=pltpu.VMEM)
    dma = pltpu.SemaphoreType.DMA
    kept = panel.dtype
    return tuple(pl.pallas_call(
        functools.partial(kernel, rows, cols),
        out_shape=(
            jax.ShapeDtypeStruct(panel.shape, kept),
            jax.ShapeDtypeStruct((tiles, per, width, width), kept),
        ),
        in_specs=[pl.BlockSpec(memory_space=pltpu.HBM)] * 3,
        out_specs=(vmem, vmem),
        scratch_shapes=[
            pltpu.SMEM(ranks.shape, ranks.dtype),
            pltpu.VMEM(panel.shape, kept),
            pltpu.VMEM((cols, order, fc), kept),
            pltpu.VMEM((tiles, order, width), kept),
            pltpu.VMEM((per, order, width), kept),
            pltpu.VMEM((tiles * width, order), kept),
            pltpu.VMEM((tiles * width, order), kept),
            pltpu.VMEM((rows, tiles * width, fr), kept),
            pltpu.VMEM((per, tiles * width, width), jnp.float32),
            dma((cols, items)),
            dma((cols // 2, items, len(FLIPS))),
            dma((rows, 2)),
            dma((cols, per)),
            dma((cols, per, 2)),
            dma((cols, per)),
            dma((3,)),
        ],
        compiler_params=pltpu.CompilerParams(
            collective_id=0, has_side_effects=True, vmem_limit_bytes=40 * 2**20
        ),
    )(ranks, panel, factor))


def solution(mesh):
    return jax.shard_map(
        functools.partial(on_device, mesh.shape["row"], mesh.shape["col"]),
        mesh=mesh,
        in_specs=(P("row", "col", None), P("row", "col"), P()),
        out_specs=(P("row", "col", None), P("row", "col", None, None)),
        check_vma=False,
    )
```

```python
import functools

import jax
import jax.numpy as jnp
from jax import lax
from jax.experimental import pallas as pl
from jax.experimental.pallas import tpu as pltpu
from jax.sharding import PartitionSpec as P

MESH = pl.DeviceIdType.MESH
FLIPS = (1, 2, 4)


def spread(value, axis, source):
    kept = jnp.where(lax.axis_index(axis) == source, value, 0).astype(value.dtype)
    return lax.psum(kept, axis)


def per_device(panel, inverse_factor, ranks):
    tile_count = panel.shape[0]
    row_part = panel.shape[1]
    rank_width = panel.shape[2]
    row_index = lax.axis_index("row")
    col_index = lax.axis_index("col")
    col_count = lax.axis_size("col")
    row_count = lax.axis_size("row")
    factor_cols = lax.all_gather(inverse_factor, "row", axis=0, tiled=True)
    own_ranks = lax.dynamic_slice_in_dim(ranks, row_index * tile_count, tile_count, 0)
    column_ids = jnp.arange(rank_width, dtype=jnp.int32)
    keep_cols = (column_ids[None, :] < own_ranks[:, None]).astype(jnp.bfloat16)
    masked = panel * keep_cols[:, None, :]
    partial_value = jnp.einsum(
        "ab,tbr->tar", factor_cols, masked, preferred_element_type=jnp.float32
    )
    summed = lax.psum(partial_value.astype(jnp.bfloat16), "col")
    solved_own = lax.dynamic_slice_in_dim(summed, col_index * row_part, row_part, 1)
    tiles_per_col = tile_count * row_count // col_count
    first_tile = col_index * tiles_per_col
    source = first_tile // tile_count
    offset = first_tile % tile_count
    picked = lax.dynamic_slice_in_dim(summed, offset, tiles_per_col, 0)
    col_tiles = spread(picked, "row", source)
    core_blocks = jnp.einsum(
        "tar,uas->turs", summed, col_tiles, preferred_element_type=jnp.float32
    ).astype(jnp.bfloat16)
    return (solved_own, core_blocks)


def kernel(
    rows, cols, ranks_hbm, p_hbm, f_hbm, o_ref, core_ref,
    ranks_ref, p_ref, fb, pb, cb, pt, srt, wt, acc,
    recv, send, zf_send, zc_recv, zc_send, loc, fetch,
):
    z = lax.axis_index("row")
    c = lax.axis_index("col")
    tiles, pr, width = p_ref.shape
    fr, fc = f_hbm.shape
    per = tiles * rows // cols
    groups = tiles // per
    source = (c * per) // tiles
    group = ((c * per) % tiles) // per

    def at(m):
        out = c
        for bit in FLIPS:
            if (m // bit) % 2:
                out = out + bit * (1 - 2 * ((c // bit) % 2))
        return out

    up, down = z + 1 < rows, z >= 1

    fetches = (
        pltpu.make_async_copy(ranks_hbm, ranks_ref, fetch.at[0]),
        pltpu.make_async_copy(
            f_hbm,
            fb.at[c, pl.ds(pl.multiple_of(z * fr, fr), fr)],
            fetch.at[1],
        ),
        pltpu.make_async_copy(p_hbm, p_ref, fetch.at[2]),
    )
    for copy in fetches:
        copy.start()

    barrier = pltpu.get_barrier_semaphore()
    for bit in FLIPS:
        pl.semaphore_signal(barrier, inc=1, device_id=(z, at(bit)), device_id_type=MESH)

    @pl.when(up)
    def _():
        pl.semaphore_signal(barrier, inc=1, device_id=(z + 1, c), device_id_type=MESH)

    @pl.when(down)
    def _():
        pl.semaphore_signal(barrier, inc=1, device_id=(z - 1, c), device_id_type=MESH)

    def f_view(s, j):
        return fb.at[s, pl.ds(pl.multiple_of(j * fr, fr), fr)]

    def p_view(s, g):
        return pb.at[pl.ds(g * per, per), pl.ds(pl.multiple_of(s * pr, pr), pr), :]

    def p_tile(s, u):
        return pb.at[group * per + u, pl.ds(pl.multiple_of(s * pr, pr), pr), :]

    def c_tile(s, u):
        return cb.at[u, pl.ds(pl.multiple_of(s * pr, pr), pr), :]

    def exists(s, j):
        return (j + 1) * fr > s * fc

    def flip_copy(view, m, item, way):
        return pltpu.make_async_remote_copy(
            src_ref=view, dst_ref=view,
            send_sem=send.at[m // 2, item, way], recv_sem=recv.at[m ^ FLIPS[way], item],
            device_id=(z, at(FLIPS[way])), device_id_type=MESH,
        )

    def act(copy, start):
        if start:
            copy.start()
        else:
            copy.wait_send()

    def wait_recv(view, m, item):
        pltpu.make_async_remote_copy(
            src_ref=view, dst_ref=view,
            send_sem=send.at[0, item, 0], recv_sem=recv.at[m, item],
            device_id=(z, at(1)), device_id_type=MESH,
        ).wait_recv()

    def f_forward(m, j, start=True):
        view = f_view(at(m), j)
        if m == 0:
            act(flip_copy(view, m, j, 1), start)
            act(flip_copy(view, m, j, 2), start)
        elif m == 2:
            @pl.when(j % 2 == 0)
            def _():
                act(flip_copy(view, m, j, 2), start)
        elif m == 4:
            @pl.when(j % 2 == 1)
            def _():
                act(flip_copy(view, m, j, 1), start)
        act(flip_copy(view, m, j, 0), start)

    def p_forward(m, g, start=True):
        view = p_view(at(m), g)
        item = rows + g
        if m == 0:
            act(flip_copy(view, m, item, 1), start)
            act(flip_copy(view, m, item, 2), start)
        elif m == 2 and g % 2 == 0:
            act(flip_copy(view, m, item, 2), start)
        elif m == 4 and g % 2 == 1:
            act(flip_copy(view, m, item, 1), start)
        act(flip_copy(view, m, item, 0), start)

    def zf(j, start=True):
        view = f_view(c, j)
        for way, (go, to) in enumerate((((z >= j) & up, z + 1), ((z <= j) & down, z - 1))):
            @pl.when(go)
            def _():
                act(pltpu.make_async_remote_copy(
                    src_ref=view, dst_ref=view,
                    send_sem=zf_send.at[j, way], recv_sem=recv.at[0, j],
                    device_id=(to, c), device_id_type=MESH,
                ), start)

    def zc(m, u, view, start=True):
        for way, (go, to) in enumerate((((z >= source) & up, z + 1), ((z <= source) & down, z - 1))):
            @pl.when(go)
            def _():
                act(pltpu.make_async_remote_copy(
                    src_ref=view, dst_ref=c_tile(at(m), u),
                    send_sem=zc_send.at[m, u, way], recv_sem=zc_recv.at[m, u],
                    device_id=(to, c), device_id_type=MESH,
                ), start)

    def own_copy(m, u):
        return pltpu.make_async_copy(p_tile(at(m), u), c_tile(at(m), u), loc.at[m, u])

    def from_source(m):
        @pl.when(z == source)
        def _():
            for u in range(per):
                zc(m, u, p_tile(at(m), u))
            for u in range(per):
                own_copy(m, u).start()

    def relay(m):
        @pl.when(z != source)
        def _():
            for u in range(per):
                view = c_tile(at(m), u)
                pltpu.make_async_remote_copy(
                    src_ref=view, dst_ref=view,
                    send_sem=zc_send.at[m, u, 0], recv_sem=zc_recv.at[m, u],
                    device_id=(z, at(1)), device_id_type=MESH,
                ).wait_recv()
                zc(m, u, view)

    for copy in fetches:
        copy.wait()
    lanes = lax.broadcasted_iota(jnp.int32, (pr, width), 1)
    for t in range(tiles):
        keep = lanes < ranks_ref[z * tiles + t]
        pb[t, pl.ds(pl.multiple_of(c * pr, pr), pr), :] = jnp.where(
            keep, p_ref[t].astype(jnp.float32), 0.0
        ).astype(pb.dtype)

    pl.semaphore_wait(barrier, len(FLIPS) + jnp.where(up, 1, 0) + jnp.where(down, 1, 0))

    @pl.when(exists(c, z))
    def _():
        zf(z)
        f_forward(0, z)

    from_source(0)
    for g in range(groups):
        p_forward(0, g)

    def near_first(body):
        for d in range(1, rows):
            for j in (z + d, z - d):
                @pl.when((j >= 0) & (j < rows))
                def _():
                    @pl.when(exists(c, j))
                    def _():
                        body(j)

    def f_along(j):
        wait_recv(f_view(c, j), 0, j)
        zf(j)
        f_forward(0, j)

    near_first(f_along)

    def p_arrive(m):
        for g in range(groups):
            wait_recv(p_view(at(m), g), m, rows + g)
            if m % 2 == 0:
                p_forward(m, g)
        from_source(m)

    def f_arrive(m):
        def one(d, carry):
            j = (z + d) % rows

            @pl.when(exists(at(m), j))
            def _():
                wait_recv(f_view(at(m), j), m, j)
                if m % 2 == 0:
                    f_forward(m, j)

            return carry

        lax.fori_loop(0, rows, one, 0)

    def flip(m):
        s = at(m)
        for t in range(tiles):
            piece = pb[t, pl.ds(pl.multiple_of(s * pr, pr), pr), :]
            pt[t * width : (t + 1) * width, pl.ds(pl.multiple_of(s * pr, pr), pr)] = piece.T

    def solve_rows(i):
        high = (i + 1) * fr
        srt[:, i * fr : high] = lax.dot_general(
            pt[:, :high],
            jnp.concatenate([fb[k, i * fr : high] for k in range(high // fc)], axis=1),
            (((1,), (1,)), ((), ())),
            preferred_element_type=jnp.float32,
        ).astype(srt.dtype)

    def weigh(i):
        wt[i] = jnp.dot(
            srt[:, i * fr :],
            jnp.concatenate(
                [fb[k, i * fr :] for k in range(i * fr // fc, (i + 1) * fr // fc)], axis=1
            ),
            preferred_element_type=jnp.float32,
        ).astype(wt.dtype)

    pieces = fr // pr
    last = cols - pieces

    def add_cores(m):
        q = at(m) // pieces

        @pl.when(z == source)
        def _():
            for k in range(pieces):
                for u in range(per):
                    own_copy(m + k, u).wait()

        for u in range(per):
            part = jnp.dot(
                wt[q], cb[u, pl.ds(pl.multiple_of(q * fr, fr), fr), :],
                preferred_element_type=jnp.float32,
            )
            if m == 0:
                acc[u] = part
            elif m < last:
                acc[u] += part
            else:
                total = (acc[u] + part).astype(core_ref.dtype)
                for t in range(tiles):
                    core_ref[t, u] = total[t * width : (t + 1) * width]

    flip(0)
    p_arrive(1)
    relay(0)
    flip(1)
    p_arrive(2)
    p_arrive(4)
    relay(1)
    p_arrive(3)
    f_arrive(2)
    f_arrive(4)
    relay(2)
    for m in (2, 3, 4):
        flip(m)
    p_arrive(5)
    p_arrive(6)
    f_arrive(6)
    relay(4)
    flip(5)
    flip(6)
    p_arrive(7)
    flip(7)
    for m in (1, 3, 5, 7):
        f_arrive(m)
    relay(3)
    for i in range(rows):
        solve_rows(i)
        if i == rows // 2 - 1:
            relay(5)
    for t in range(tiles):
        o_ref[t] = srt[t * width : (t + 1) * width, pl.ds(pl.multiple_of(c * pr, pr), pr)].T
    relay(6)
    for i in range(rows):
        weigh(i)
    passes = ((z > source) & up) | ((z < source) & down)

    def add_early():
        for m in range(0, last, pieces):
            add_cores(m)

    pl.when(jnp.logical_not(passes))(add_early)
    relay(7)
    pl.when(passes)(add_early)
    add_cores(last)

    @pl.when(exists(c, z))
    def _():
        zf(z, start=False)
        f_forward(0, z, start=False)

    def f_along_left(j):
        zf(j, start=False)
        f_forward(0, j, start=False)

    near_first(f_along_left)
    for m in range(0, cols, 2):
        for g in range(groups):
            p_forward(m, g, start=False)
        if m:
            def one(j, carry, m=m):
                @pl.when(exists(at(m), j))
                def _():
                    f_forward(m, j, start=False)

                return carry

            lax.fori_loop(0, rows, one, 0)
    for m in range(cols):
        for u in range(per):
            @pl.when(z == source)
            def _():
                zc(m, u, p_tile(at(m), u), start=False)

            @pl.when(z != source)
            def _():
                zc(m, u, c_tile(at(m), u), start=False)


def fits(rows, cols, panel, factor):
    tiles, pr, width = panel.shape
    fr, fc = factor.shape
    per = tiles * rows // cols
    return (
        cols == 2 ** len(FLIPS)
        and rows > 1
        and per > 0
        and tiles == 2 * per
        and pr == fc
        and pr % 16 == 0
        and fr == 2 * fc
        and fc % 128 == 0
        and width % 128 == 0
        and rows * fr == cols * fc
    )


def on_device(rows, cols, panel, factor, ranks):
    if not fits(rows, cols, panel, factor):
        return per_device(panel, factor, ranks)
    tiles, pr, width = panel.shape
    fr, fc = factor.shape
    order = rows * fr
    per = tiles * rows // cols
    items = rows + tiles // per
    vmem = pl.BlockSpec(memory_space=pltpu.VMEM)
    dma = pltpu.SemaphoreType.DMA
    kept = panel.dtype
    return tuple(pl.pallas_call(
        functools.partial(kernel, rows, cols),
        out_shape=(
            jax.ShapeDtypeStruct(panel.shape, kept),
            jax.ShapeDtypeStruct((tiles, per, width, width), kept),
        ),
        in_specs=[pl.BlockSpec(memory_space=pltpu.HBM)] * 3,
        out_specs=(vmem, vmem),
        scratch_shapes=[
            pltpu.SMEM(ranks.shape, ranks.dtype),
            pltpu.VMEM(panel.shape, kept),
            pltpu.VMEM((cols, order, fc), kept),
            pltpu.VMEM((tiles, order, width), kept),
            pltpu.VMEM((per, order, width), kept),
            pltpu.VMEM((tiles * width, order), kept),
            pltpu.VMEM((tiles * width, order), kept),
            pltpu.VMEM((rows, tiles * width, fr), kept),
            pltpu.VMEM((per, tiles * width, width), jnp.float32),
            dma((cols, items)),
            dma((cols // 2, items, len(FLIPS))),
            dma((rows, 2)),
            dma((cols, per)),
            dma((cols, per, 2)),
            dma((cols, per)),
            dma((3,)),
        ],
        compiler_params=pltpu.CompilerParams(
            collective_id=0, has_side_effects=True, vmem_limit_bytes=40 * 2**20
        ),
    )(ranks, panel, factor))


def solution(mesh):
    return jax.shard_map(
        functools.partial(on_device, mesh.shape["row"], mesh.shape["col"]),
        mesh=mesh,
        in_specs=(P("row", "col", None), P("row", "col"), P()),
        out_specs=(P("row", "col", None), P("row", "col", None, None)),
        check_vma=False,
    )
```

```python
import functools

import jax
import jax.numpy as jnp
from jax import lax
from jax.experimental import pallas as pl
from jax.experimental.pallas import tpu as pltpu
from jax.sharding import PartitionSpec as P

MESH = pl.DeviceIdType.MESH
FLIPS = (1, 2, 4)


def spread(value, axis, source):
    kept = jnp.where(lax.axis_index(axis) == source, value, 0).astype(value.dtype)
    return lax.psum(kept, axis)


def per_device(panel, inverse_factor, ranks):
    tile_count = panel.shape[0]
    row_part = panel.shape[1]
    rank_width = panel.shape[2]
    row_index = lax.axis_index("row")
    col_index = lax.axis_index("col")
    col_count = lax.axis_size("col")
    row_count = lax.axis_size("row")
    factor_cols = lax.all_gather(inverse_factor, "row", axis=0, tiled=True)
    own_ranks = lax.dynamic_slice_in_dim(ranks, row_index * tile_count, tile_count, 0)
    column_ids = jnp.arange(rank_width, dtype=jnp.int32)
    keep_cols = (column_ids[None, :] < own_ranks[:, None]).astype(jnp.bfloat16)
    masked = panel * keep_cols[:, None, :]
    partial_value = jnp.einsum(
        "ab,tbr->tar", factor_cols, masked, preferred_element_type=jnp.float32
    )
    summed = lax.psum(partial_value.astype(jnp.bfloat16), "col")
    solved_own = lax.dynamic_slice_in_dim(summed, col_index * row_part, row_part, 1)
    tiles_per_col = tile_count * row_count // col_count
    first_tile = col_index * tiles_per_col
    source = first_tile // tile_count
    offset = first_tile % tile_count
    picked = lax.dynamic_slice_in_dim(summed, offset, tiles_per_col, 0)
    col_tiles = spread(picked, "row", source)
    core_blocks = jnp.einsum(
        "tar,uas->turs", summed, col_tiles, preferred_element_type=jnp.float32
    ).astype(jnp.bfloat16)
    return (solved_own, core_blocks)


def kernel(
    rows, cols, ranks_hbm, p_hbm, f_hbm, o_ref, core_ref,
    ranks_ref, p_ref, fb, pb, cb, pt, srt, wt, acc,
    recv, send, zf_send, zc_recv, zc_send, loc, fetch,
):
    z = lax.axis_index("row")
    c = lax.axis_index("col")
    tiles, pr, width = p_ref.shape
    fr, fc = f_hbm.shape
    per = tiles * rows // cols
    groups = tiles // per
    source = (c * per) // tiles
    group = ((c * per) % tiles) // per

    def at(m):
        out = c
        for bit in FLIPS:
            if (m // bit) % 2:
                out = out + bit * (1 - 2 * ((c // bit) % 2))
        return out

    up, down = z + 1 < rows, z >= 1

    fetches = (
        pltpu.make_async_copy(ranks_hbm, ranks_ref, fetch.at[0]),
        pltpu.make_async_copy(
            f_hbm,
            fb.at[c, pl.ds(pl.multiple_of(z * fr, fr), fr)],
            fetch.at[1],
        ),
        pltpu.make_async_copy(p_hbm, p_ref, fetch.at[2]),
    )
    for copy in fetches:
        copy.start()

    barrier = pltpu.get_barrier_semaphore()
    for bit in FLIPS:
        pl.semaphore_signal(barrier, inc=1, device_id=(z, at(bit)), device_id_type=MESH)

    @pl.when(up)
    def _():
        pl.semaphore_signal(barrier, inc=1, device_id=(z + 1, c), device_id_type=MESH)

    @pl.when(down)
    def _():
        pl.semaphore_signal(barrier, inc=1, device_id=(z - 1, c), device_id_type=MESH)

    def f_view(s, j):
        return fb.at[s, pl.ds(pl.multiple_of(j * fr, fr), fr)]

    def p_view(s, g):
        return pb.at[pl.ds(g * per, per), pl.ds(pl.multiple_of(s * pr, pr), pr), :]

    def p_tile(s, u):
        return pb.at[group * per + u, pl.ds(pl.multiple_of(s * pr, pr), pr), :]

    def c_tile(s, u):
        return cb.at[u, pl.ds(pl.multiple_of(s * pr, pr), pr), :]

    def exists(s, j):
        return (j + 1) * fr > s * fc

    def flip_copy(view, m, item, way):
        return pltpu.make_async_remote_copy(
            src_ref=view, dst_ref=view,
            send_sem=send.at[m // 2, item, way], recv_sem=recv.at[m ^ FLIPS[way], item],
            device_id=(z, at(FLIPS[way])), device_id_type=MESH,
        )

    def act(copy, start):
        if start:
            copy.start()
        else:
            copy.wait_send()

    def wait_recv(view, m, item):
        pltpu.make_async_remote_copy(
            src_ref=view, dst_ref=view,
            send_sem=send.at[0, item, 0], recv_sem=recv.at[m, item],
            device_id=(z, at(1)), device_id_type=MESH,
        ).wait_recv()

    def f_forward(m, j, start=True):
        view = f_view(at(m), j)
        if m == 0:
            act(flip_copy(view, m, j, 1), start)
            act(flip_copy(view, m, j, 2), start)
        elif m == 2:
            @pl.when(j % 2 == 0)
            def _():
                act(flip_copy(view, m, j, 2), start)
        elif m == 4:
            @pl.when(j % 2 == 1)
            def _():
                act(flip_copy(view, m, j, 1), start)
        act(flip_copy(view, m, j, 0), start)

    def p_forward(m, g, start=True):
        view = p_view(at(m), g)
        item = rows + g
        if m == 0:
            act(flip_copy(view, m, item, 1), start)
            act(flip_copy(view, m, item, 2), start)
        elif m == 2 and g % 2 == 0:
            act(flip_copy(view, m, item, 2), start)
        elif m == 4 and g % 2 == 1:
            act(flip_copy(view, m, item, 1), start)
        act(flip_copy(view, m, item, 0), start)

    def zf(j, start=True):
        view = f_view(c, j)
        for way, (go, to) in enumerate((((z >= j) & up, z + 1), ((z <= j) & down, z - 1))):
            @pl.when(go)
            def _():
                act(pltpu.make_async_remote_copy(
                    src_ref=view, dst_ref=view,
                    send_sem=zf_send.at[j, way], recv_sem=recv.at[0, j],
                    device_id=(to, c), device_id_type=MESH,
                ), start)

    def zc(m, u, view, start=True):
        for way, (go, to) in enumerate((((z >= source) & up, z + 1), ((z <= source) & down, z - 1))):
            @pl.when(go)
            def _():
                act(pltpu.make_async_remote_copy(
                    src_ref=view, dst_ref=c_tile(at(m), u),
                    send_sem=zc_send.at[m, u, way], recv_sem=zc_recv.at[m, u],
                    device_id=(to, c), device_id_type=MESH,
                ), start)

    def own_copy(m, u):
        return pltpu.make_async_copy(p_tile(at(m), u), c_tile(at(m), u), loc.at[m, u])

    def from_source(m):
        @pl.when(z == source)
        def _():
            for u in range(per):
                zc(m, u, p_tile(at(m), u))
            for u in range(per):
                own_copy(m, u).start()

    def relay(m):
        @pl.when(z != source)
        def _():
            for u in range(per):
                view = c_tile(at(m), u)
                pltpu.make_async_remote_copy(
                    src_ref=view, dst_ref=view,
                    send_sem=zc_send.at[m, u, 0], recv_sem=zc_recv.at[m, u],
                    device_id=(z, at(1)), device_id_type=MESH,
                ).wait_recv()
                zc(m, u, view)

    for copy in fetches:
        copy.wait()
    lanes = lax.broadcasted_iota(jnp.int32, (pr, width), 1)
    for t in range(tiles):
        keep = lanes < ranks_ref[z * tiles + t]
        pb[t, pl.ds(pl.multiple_of(c * pr, pr), pr), :] = jnp.where(
            keep, p_ref[t].astype(jnp.float32), 0.0
        ).astype(pb.dtype)

    pl.semaphore_wait(barrier, len(FLIPS) + jnp.where(up, 1, 0) + jnp.where(down, 1, 0))

    @pl.when(exists(c, z))
    def _():
        zf(z)

    from_source(0)
    for g in range(groups):
        p_forward(0, g)

    @pl.when(exists(c, z))
    def _():
        f_forward(0, z)

    def near_first(body):
        for d in range(1, rows):
            for j in (z + d, z - d):
                @pl.when((j >= 0) & (j < rows))
                def _():
                    @pl.when(exists(c, j))
                    def _():
                        body(j)

    def f_along(j):
        wait_recv(f_view(c, j), 0, j)
        zf(j)
        f_forward(0, j)

    near_first(f_along)

    def p_arrive(m):
        for g in range(groups):
            wait_recv(p_view(at(m), g), m, rows + g)
            if m % 2 == 0:
                p_forward(m, g)
        from_source(m)

    def f_arrive(m):
        def one(d, carry):
            j = (z + d) % rows

            @pl.when(exists(at(m), j))
            def _():
                wait_recv(f_view(at(m), j), m, j)
                if m % 2 == 0:
                    f_forward(m, j)

            return carry

        lax.fori_loop(0, rows, one, 0)

    def flip(m):
        s = at(m)
        for t in range(tiles):
            piece = pb[t, pl.ds(pl.multiple_of(s * pr, pr), pr), :]
            pt[t * width : (t + 1) * width, pl.ds(pl.multiple_of(s * pr, pr), pr)] = piece.T

    def solve_rows(i):
        high = (i + 1) * fr
        srt[:, i * fr : high] = lax.dot_general(
            pt[:, :high],
            jnp.concatenate([fb[k, i * fr : high] for k in range(high // fc)], axis=1),
            (((1,), (1,)), ((), ())),
            preferred_element_type=jnp.float32,
        ).astype(srt.dtype)

    def weigh(i):
        wt[i] = jnp.dot(
            srt[:, i * fr :],
            jnp.concatenate(
                [fb[k, i * fr :] for k in range(i * fr // fc, (i + 1) * fr // fc)], axis=1
            ),
            preferred_element_type=jnp.float32,
        ).astype(wt.dtype)

    pieces = fr // pr
    last = cols - pieces

    def add_cores(m):
        q = at(m) // pieces

        @pl.when(z == source)
        def _():
            for k in range(pieces):
                for u in range(per):
                    own_copy(m + k, u).wait()

        for u in range(per):
            part = jnp.dot(
                wt[q], cb[u, pl.ds(pl.multiple_of(q * fr, fr), fr), :],
                preferred_element_type=jnp.float32,
            )
            if m == 0:
                acc[u] = part
            elif m < last:
                acc[u] += part
            else:
                total = (acc[u] + part).astype(core_ref.dtype)
                for t in range(tiles):
                    core_ref[t, u] = total[t * width : (t + 1) * width]

    flip(0)
    p_arrive(1)
    relay(0)
    flip(1)
    p_arrive(2)
    p_arrive(4)
    relay(1)
    p_arrive(3)
    f_arrive(2)
    f_arrive(4)
    relay(2)
    for m in (2, 3, 4):
        flip(m)
    p_arrive(5)
    p_arrive(6)
    f_arrive(6)
    relay(4)
    flip(5)
    flip(6)
    p_arrive(7)
    flip(7)
    for m in (1, 3, 5, 7):
        f_arrive(m)
    relay(3)
    for i in range(rows):
        solve_rows(i)
        if i == rows // 2 - 1:
            relay(5)
    for t in range(tiles):
        o_ref[t] = srt[t * width : (t + 1) * width, pl.ds(pl.multiple_of(c * pr, pr), pr)].T
    relay(6)
    for i in range(rows):
        weigh(i)
    passes = ((z > source) & up) | ((z < source) & down)

    def add_early():
        for m in range(0, last, pieces):
            add_cores(m)

    pl.when(jnp.logical_not(passes))(add_early)
    relay(7)
    pl.when(passes)(add_early)
    add_cores(last)

    @pl.when(exists(c, z))
    def _():
        zf(z, start=False)
        f_forward(0, z, start=False)

    def f_along_left(j):
        zf(j, start=False)
        f_forward(0, j, start=False)

    near_first(f_along_left)
    for m in range(0, cols, 2):
        for g in range(groups):
            p_forward(m, g, start=False)
        if m:
            def one(j, carry, m=m):
                @pl.when(exists(at(m), j))
                def _():
                    f_forward(m, j, start=False)

                return carry

            lax.fori_loop(0, rows, one, 0)
    for m in range(cols):
        for u in range(per):
            @pl.when(z == source)
            def _():
                zc(m, u, p_tile(at(m), u), start=False)

            @pl.when(z != source)
            def _():
                zc(m, u, c_tile(at(m), u), start=False)


def fits(rows, cols, panel, factor):
    tiles, pr, width = panel.shape
    fr, fc = factor.shape
    per = tiles * rows // cols
    return (
        cols == 2 ** len(FLIPS)
        and rows > 1
        and per > 0
        and tiles == 2 * per
        and pr == fc
        and pr % 16 == 0
        and fr == 2 * fc
        and fc % 128 == 0
        and width % 128 == 0
        and rows * fr == cols * fc
    )


def on_device(rows, cols, panel, factor, ranks):
    if not fits(rows, cols, panel, factor):
        return per_device(panel, factor, ranks)
    tiles, pr, width = panel.shape
    fr, fc = factor.shape
    order = rows * fr
    per = tiles * rows // cols
    items = rows + tiles // per
    vmem = pl.BlockSpec(memory_space=pltpu.VMEM)
    dma = pltpu.SemaphoreType.DMA
    kept = panel.dtype
    return tuple(pl.pallas_call(
        functools.partial(kernel, rows, cols),
        out_shape=(
            jax.ShapeDtypeStruct(panel.shape, kept),
            jax.ShapeDtypeStruct((tiles, per, width, width), kept),
        ),
        in_specs=[pl.BlockSpec(memory_space=pltpu.HBM)] * 3,
        out_specs=(vmem, vmem),
        scratch_shapes=[
            pltpu.SMEM(ranks.shape, ranks.dtype),
            pltpu.VMEM(panel.shape, kept),
            pltpu.VMEM((cols, order, fc), kept),
            pltpu.VMEM((tiles, order, width), kept),
            pltpu.VMEM((per, order, width), kept),
            pltpu.VMEM((tiles * width, order), kept),
            pltpu.VMEM((tiles * width, order), kept),
            pltpu.VMEM((rows, tiles * width, fr), kept),
            pltpu.VMEM((per, tiles * width, width), jnp.float32),
            dma((cols, items)),
            dma((cols // 2, items, len(FLIPS))),
            dma((rows, 2)),
            dma((cols, per)),
            dma((cols, per, 2)),
            dma((cols, per)),
            dma((3,)),
        ],
        compiler_params=pltpu.CompilerParams(
            collective_id=0, has_side_effects=True, vmem_limit_bytes=40 * 2**20
        ),
    )(ranks, panel, factor))


def solution(mesh):
    return jax.shard_map(
        functools.partial(on_device, mesh.shape["row"], mesh.shape["col"]),
        mesh=mesh,
        in_specs=(P("row", "col", None), P("row", "col"), P()),
        out_specs=(P("row", "col", None), P("row", "col", None, None)),
        check_vma=False,
    )
```
